128 devices in a mesh: grp: 4 (over x_lo, core), tp: 32 (over y, x_hi, z).
Axes of the slice: x: 4 (x_hi: 2, x_lo: 2; x = x_hi * 2 + x_lo), y: 4, z: 4, core: 2. Of those that a mesh axis runs over, the one named last changes fastest.
Arguments:
- queries: bfloat16 [128, 16, 2048], P(('grp', 'tp')), may hold values from -36 to 36
- cache_keys: bfloat16 [128, 16, 2048, 128], P(('grp', 'tp')), may hold values from -7.5 to 7.5
- cache_values: bfloat16 [128, 16, 2048, 128], P(('grp', 'tp')), may hold values from -24 to 24
- lengths: int32 [256], replicated, may hold values from 512 to 2048
- old_tiles: bfloat16 [128, 128, 128, 128], P(('grp', 'tp')), may hold values from -0.046875 to 0.046875
- old_scales: bfloat16 [128, 128, 128], P(('grp', 'tp')), may hold values from 0.29882812 to 3
- slot_tiles: int32 [128, 128], replicated, may hold values from 0 to 16383, as said below
Outputs:
- projected: bfloat16 [256, 16384], P('tp', 'grp')
The draws below stay inside these ranges and needn't reach their ends.
Inputs may be any that keep to these rules, and one draw needn't show every extreme that they name: Each row of slot_tiles names exactly one tile of each new owner n (tile numbers n * 128 to n * 128 + 127), and every tile number stands exactly once in the whole table.
All inputs are finite; a program needn't handle non-finite values.
Results may differ from the reference program's by a relative error of at most 0.03.
Values may be sent and summed in bfloat16 or wider, within the bound.
A program may use at most 128 MiB of HBM per device.

```python
import math
import jax
import jax.numpy as jnp
from jax import lax

D = 16384
KV_HEADS = 8
HEAD_DIM = 128
GROUP_ROWS = 16
CACHE_LEN = 2048
TILE_COLS = 128
ALL_DEVICES = 128
GROUP_HEADS = 16
FEAT_SLICE = 64
BLOCK_COLS = 4096
COL_TILES = 32
ROW_TILES = 4
TILE_ROWS = 128
ROWS = 256
N_GRP = 4
N_TP = 32


def draw_queries(key, part):
    key = jax.random.fold_in(key, 7)
    result = jnp.clip(jax.random.normal(key, (ALL_DEVICES, GROUP_ROWS, GROUP_HEADS * HEAD_DIM), jnp.float32), -6.0, 6.0)
    return result.astype(jnp.bfloat16)


def draw_cache_keys(key, part):
    key = jax.random.fold_in(key, 5)
    result = jnp.clip(jax.random.normal(key, (ALL_DEVICES, GROUP_ROWS, CACHE_LEN, HEAD_DIM), jnp.float32), -6.0, 6.0)
    return result.astype(jnp.bfloat16)


def draw_lengths(key, part):
    key = jax.random.fold_in(key, 9)
    result = jax.random.randint(key, (ROWS,), max(CACHE_LEN // 4, 2), CACHE_LEN + 1, dtype=jnp.int32)
    return result.at[0].set(CACHE_LEN)


def permute_one(subkey):
    return jax.random.permutation(subkey, ALL_DEVICES).astype(jnp.int32)


def draw_slot_tiles(key, part):
    key = jax.random.fold_in(key, 13)
    first_key, second_key = jax.random.split(key)
    owner_perms = jax.vmap(permute_one)(jax.random.split(first_key, ALL_DEVICES))
    slot_perms = jax.vmap(permute_one)(jax.random.split(second_key, ALL_DEVICES))
    local_ids = jnp.take_along_axis(owner_perms.T, slot_perms, axis=1)
    return (slot_perms * ALL_DEVICES + local_ids).astype(jnp.int32)


def steps_of(rng, dims, shards, smallest, largest):
    def one(dim, shards_of):
        heights = jax.random.uniform(jax.random.fold_in(jax.random.fold_in(rng, 6), dim), (shards_of,), jnp.float32, smallest / len(shards), largest / len(shards))
        return jnp.repeat(jnp.exp(heights), dims[dim] // shards_of).reshape((-1,) + (1,) * (len(dims) - dim - 1))

    gain = one(*shards[0])
    for cut in shards[1:]:
        gain = gain * one(*cut)
    return gain


def normal_values(rng, extent, scale, most, shards=(), kind=jnp.bfloat16):
    loudness = steps_of(rng, extent, shards, -0.22, 0.18) if shards else 1.0
    values = jax.random.normal(rng, extent, jnp.float32) * scale * loudness
    return jnp.minimum(jnp.maximum(values, -most), most).astype(kind)


def setup_inputs(seed: int = 0) -> dict:
    splits = jax.random.split(jax.random.key(seed), 8)
    queries = draw_queries(jax.random.fold_in(splits[7], 71), 0)
    cache_keys = draw_cache_keys(jax.random.fold_in(splits[7], 71), 0)
    cache_values = normal_values(splits[2], (ALL_DEVICES, GROUP_ROWS, CACHE_LEN, HEAD_DIM), 4.0, 24.0, ((0, 128),))
    lengths = draw_lengths(jax.random.fold_in(splits[7], 71), 0)
    old_tiles = normal_values(splits[4], (ALL_DEVICES, ALL_DEVICES, TILE_ROWS, TILE_COLS), D ** -0.5, 0.046875, ((0, 128),))
    old_scales = jnp.clip(jnp.exp(math.log(3.0) - 2.306499 * jax.random.uniform(splits[5], (ALL_DEVICES, ALL_DEVICES, TILE_ROWS), jnp.float32) ** steps_of(splits[5], (ALL_DEVICES, ALL_DEVICES, TILE_ROWS), ((0, 128),), -0.2, 0.2)), 0.29882812, 3.0).astype(jnp.bfloat16)
    slot_tiles = draw_slot_tiles(jax.random.fold_in(splits[7], 71), 0)
    return {"queries": queries, "cache_keys": cache_keys, "cache_values": cache_values, "lengths": lengths, "old_tiles": old_tiles, "old_scales": old_scales, "slot_tiles": slot_tiles}


def attend_rows(queries_one, keys_one, values_one, live_len):
    row_count = queries_one.shape[0]
    per_head = queries_one.reshape(row_count, GROUP_HEADS, HEAD_DIM).astype(jnp.float32)
    scores = jnp.einsum('rhd,rld->rhl', per_head, keys_one.astype(jnp.float32)) * (HEAD_DIM ** -0.5)
    inside = lax.broadcasted_iota(jnp.int32, scores.shape, 2) < live_len[:, None, None]
    scores = jnp.where(inside, scores, -1e30)
    row_max = jnp.max(scores, axis=2, keepdims=True)
    weights = jnp.where(inside, jnp.exp(scores - row_max), 0.0)
    row_sum = jnp.sum(weights, axis=2, keepdims=True)
    attn_weights = (weights / row_sum).astype(jnp.bfloat16)
    mixed_out = jnp.einsum('rhl,rld->rhd', attn_weights.astype(jnp.float32), values_one.astype(jnp.float32))
    return mixed_out.astype(jnp.bfloat16).reshape(row_count, GROUP_HEADS * HEAD_DIM)


def attend_packed(packed):
    return attend_rows(packed[0], packed[1], packed[2], packed[3])


def reference(queries, cache_keys, cache_values, lengths, old_tiles, old_scales, slot_tiles):
    live_all = jnp.repeat(lengths.reshape(ALL_DEVICES // KV_HEADS, GROUP_ROWS), KV_HEADS, axis=0)
    attended = lax.map(attend_packed, (queries, cache_keys, cache_values, live_all))
    features = attended.reshape(ALL_DEVICES // KV_HEADS, KV_HEADS, GROUP_ROWS, GROUP_HEADS * HEAD_DIM)
    features = features.transpose(0, 2, 1, 3).reshape(ROWS, D)
    arrange = jnp.argsort(slot_tiles.reshape(-1)).astype(jnp.int32)
    sorted_tiles = old_tiles.reshape(ALL_DEVICES * ALL_DEVICES, TILE_ROWS, TILE_COLS)[arrange]
    sorted_scales = old_scales.reshape(ALL_DEVICES * ALL_DEVICES, TILE_ROWS)[arrange]
    dequant = (sorted_tiles.astype(jnp.float32) * sorted_scales.astype(jnp.float32)[:, :, None]).astype(jnp.bfloat16)
    blocks = dequant.reshape(N_GRP, N_TP, ROW_TILES, COL_TILES, TILE_ROWS, TILE_COLS)
    blocks = blocks.transpose(0, 1, 2, 4, 3, 5).reshape(N_GRP, N_TP, KV_HEADS, FEAT_SLICE, BLOCK_COLS)
    out_weight = blocks.transpose(2, 1, 3, 0, 4).reshape(D, D)
    weight_parts = out_weight.reshape(KV_HEADS, N_TP, FEAT_SLICE, D).transpose(1, 0, 2, 3)
    weight_parts = weight_parts.reshape(N_TP, KV_HEADS * FEAT_SLICE, D)
    feature_parts = features.reshape(ROWS, KV_HEADS, N_TP, FEAT_SLICE).transpose(2, 0, 1, 3)
    feature_parts = feature_parts.reshape(N_TP, ROWS, KV_HEADS * FEAT_SLICE)

    def add_part(total, pieces):
        term = jnp.dot(pieces[0], pieces[1], preferred_element_type=jnp.float32).astype(jnp.bfloat16)
        term = lax.optimization_barrier(term)
        return total + term.astype(jnp.float32), None

    total, unused = lax.scan(add_part, jnp.zeros((ROWS, D), jnp.float32), (feature_parts, weight_parts))
    return total.astype(jnp.bfloat16)
```

```python
import jax
import jax.numpy as jnp
from jax import lax
from jax.sharding import PartitionSpec as P

D = 16384
KV_HEADS = 8
HEAD_DIM = 128
GROUP_HEADS = 16


def attend_rows(queries_one, keys_one, values_one, live_len):
    row_count = queries_one.shape[0]
    per_head = queries_one.reshape(row_count, GROUP_HEADS, HEAD_DIM)
    scores = jnp.einsum(
        "rhd,rld->rhl", per_head, keys_one, preferred_element_type=jnp.float32
    ) * HEAD_DIM ** (-0.5)
    inside = lax.broadcasted_iota(jnp.int32, scores.shape, 2) < live_len[:, None, None]
    scores = jnp.where(inside, scores, -1e30)
    row_max = jnp.max(scores, axis=2, keepdims=True)
    weights = jnp.where(inside, jnp.exp(scores - row_max), 0.0)
    row_sum = jnp.sum(weights, axis=2, keepdims=True)
    attn_weights = (weights / row_sum).astype(jnp.bfloat16)
    mixed_out = jnp.einsum(
        "rhl,rld->rhd", attn_weights, values_one, preferred_element_type=jnp.float32
    )
    return mixed_out.astype(jnp.bfloat16).reshape(row_count, GROUP_HEADS * HEAD_DIM)


def body(queries, cache_keys, cache_values, lengths, old_tiles, old_scales, slot_tiles):
    groups = lax.axis_size("grp")
    tp_count = lax.axis_size("tp")
    devices = groups * tp_count
    myself = lax.axis_index("grp") * tp_count + lax.axis_index("tp")
    group_rows = queries.shape[1]
    first_row = myself // KV_HEADS * group_rows
    live_len = lax.dynamic_slice_in_dim(lengths, first_row, group_rows)
    attended = attend_rows(queries[0], cache_keys[0], cache_values[0], live_len)
    slice_width = GROUP_HEADS * HEAD_DIM // tp_count
    pieces = attended.reshape(group_rows, tp_count, slice_width).transpose(1, 0, 2)
    pieces = jnp.broadcast_to(pieces[None], (groups, tp_count, group_rows, slice_width))
    pieces = pieces.reshape(devices, group_rows, slice_width)
    arrived = lax.all_to_all(pieces, ("grp", "tp"), split_axis=0, concat_axis=0, tiled=True)
    features = arrived.reshape(devices // KV_HEADS, KV_HEADS, group_rows, slice_width)
    features = features.transpose(0, 2, 1, 3).reshape(
        devices // KV_HEADS * group_rows, KV_HEADS * slice_width
    )
    tile_rows = old_tiles.shape[2]
    tile_cols = old_tiles.shape[3]
    my_slots = lax.dynamic_index_in_dim(slot_tiles, myself, 0, keepdims=False)
    by_owner = jnp.argsort(my_slots // devices)
    send_tiles = old_tiles[0][by_owner]
    send_scales = old_scales[0][by_owner]
    got_tiles, got_scales = (
        lax.all_to_all(send_tiles, ("grp", "tp"), split_axis=0, concat_axis=0, tiled=True),
        lax.all_to_all(send_scales, ("grp", "tp"), split_axis=0, concat_axis=0, tiled=True),
    )
    matches = slot_tiles // devices == myself
    local_index = jnp.sum(jnp.where(matches, slot_tiles % devices, 0), axis=1)
    arrange = jnp.argsort(local_index)
    placed = got_tiles[arrange]
    scales = got_scales[arrange]
    dequant = (placed.astype(jnp.float32) * scales.astype(jnp.float32)[:, :, None]).astype(
        jnp.bfloat16
    )
    block_cols = D // groups
    col_tiles = block_cols // tile_cols
    row_tiles = devices // col_tiles
    new_block = dequant.reshape(row_tiles, col_tiles, tile_rows, tile_cols).transpose(0, 2, 1, 3)
    new_block = new_block.reshape(row_tiles * tile_rows, col_tiles * tile_cols)
    product = jnp.dot(features, new_block, preferred_element_type=jnp.float32)
    terms = product.astype(jnp.bfloat16).reshape(tp_count, -1, block_cols)
    terms = lax.all_to_all(terms, "tp", split_axis=0, concat_axis=0, tiled=True)
    return jnp.sum(terms.astype(jnp.float32), axis=0).astype(jnp.bfloat16)


def solution(mesh):
    return jax.shard_map(
        body,
        mesh=mesh,
        in_specs=(
            P(("grp", "tp"), None, None),
            P(("grp", "tp"), None, None, None),
            P(("grp", "tp"), None, None, None),
            P(),
            P(("grp", "tp"), None, None, None),
            P(("grp", "tp"), None, None),
            P(),
        ),
        out_specs=P("tp", "grp"),
        check_vma=False,
    )
```

```python
import jax
import jax.numpy as jnp
from jax import lax
from jax.experimental import pallas as pl
from jax.experimental.pallas import tpu as pltpu
from jax.sharding import PartitionSpec as P

KV_HEADS = 8
HEAD_DIM = 128
HEADS = 16
LANES = 128
ORDERS = ("xyz", "yzx", "zxy")
COUNTS = (6, 5, 5)
STARTS = (0, 6, 11)
ROWS = 256
TILES = 128
MESH = pl.DeviceIdType.MESH


def attend_rows(queries_one, keys_one, values_one, live_len):
    row_count = queries_one.shape[0]
    per_head = queries_one.reshape(row_count, HEADS, HEAD_DIM)
    scores = jnp.einsum(
        "rhd,rld->rhl", per_head, keys_one, preferred_element_type=jnp.float32
    ) * HEAD_DIM ** (-0.5)
    inside = lax.broadcasted_iota(jnp.int32, scores.shape, 2) < live_len[:, None, None]
    scores = jnp.where(inside, scores, -1e30)
    row_max = jnp.max(scores, axis=2, keepdims=True)
    weights = jnp.where(inside, jnp.exp(scores - row_max), 0.0)
    row_sum = jnp.sum(weights, axis=2, keepdims=True)
    attn_weights = (weights / row_sum).astype(jnp.bfloat16)
    mixed_out = jnp.einsum(
        "rhl,rld->rhd", attn_weights, values_one, preferred_element_type=jnp.float32
    )
    return mixed_out.astype(jnp.bfloat16).transpose(1, 0, 2)


def tile_table(slot_tiles, grp, tp):
    core = grp % 2
    own = lax.dynamic_index_in_dim(slot_tiles, grp * 32 + tp, 0, keepdims=False)
    other = lax.dynamic_index_in_dim(
        slot_tiles, (grp + 1 - 2 * core) * 32 + tp, 0, keepdims=False
    )
    spot = lax.broadcasted_iota(jnp.int32, (TILES, TILES), 0)
    slot = lax.broadcasted_iota(jnp.int32, (TILES, TILES), 1)
    owner = ((spot // 2) % 2 * 2 + core) * 32 + spot // 4
    held = jnp.where(spot % 2 == 0, own[None], other[None])
    packed = slot * 128 + held % 128
    packed = jnp.sum(jnp.where(held // 128 == owner, packed, 0), axis=1)
    index = jnp.arange(TILES, dtype=jnp.int32)
    key = index // 2 % 2 * 32 + packed % 32
    before = (key[None] == key[:, None]) & (index[None] < index[:, None])
    previous = jnp.max(jnp.where(before, index[None], -1), axis=1)
    last = jnp.max(jnp.where(key[None] == index[:, None], index[None], -1), axis=1)
    return jnp.stack([packed // 128, packed % 128 // 32, previous, last])


def kernel(*refs):
    table, att, tiles_own, tiles_other, scales_own, scales_other, out = refs[:7]
    scratch = list(refs[7:])
    feats = [scratch.pop(0) for _ in range(3)]
    sends = [scratch.pop(0) for _ in range(3)]
    lands = [[[scratch.pop(0) for _ in range(4)] for _ in range(3)] for _ in range(3)]
    tiles, scales, weights, sums = [scratch.pop(0) for _ in range(4)]
    load_sem, ag_send, ag_recv, sib_send, sib_recv, rs_send, rs_recv = scratch

    grp, tp = lax.axis_index("grp"), lax.axis_index("tp")
    core = lax.rem(grp, 2)
    me = {"x": lax.rem(lax.div(tp, 4), 2) * 2 + lax.div(grp, 2), "y": lax.div(tp, 8), "z": lax.rem(tp, 4)}

    def shifted(axis, by):
        return lax.rem(me[axis] + by, 4)

    def device(axis, by):
        at = dict(me)
        at[axis] = shifted(axis, by)
        return (
            lax.rem(at["x"], 2) * 2 + core,
            at["y"] * 8 + lax.div(at["x"], 2) * 4 + at["z"],
        )

    nxt = {axis: device(axis, 1) for axis in "xyz"}
    prv = {axis: device(axis, 3) for axis in "xyz"}
    sibling = (grp + 1 - 2 * core, tp)

    loads = [
        pltpu.make_async_copy(tiles_own, tiles.at[0], load_sem.at[0]),
        pltpu.make_async_copy(tiles_other, tiles.at[1], load_sem.at[1]),
    ]
    for load in loads:
        load.start()

    barrier = pltpu.get_barrier_semaphore()
    for other in [*nxt.values(), *prv.values(), sibling]:
        pl.semaphore_signal(barrier, inc=1, device_id=other, device_id_type=MESH)
    pl.semaphore_wait(barrier, 7)

    def remote(src, dst, send, recv, target):
        return pltpu.make_async_remote_copy(
            src_ref=src, dst_ref=dst, send_sem=send, recv_sem=recv,
            device_id=target, device_id_type=MESH,
        )

    pending = []

    def go(copy):
        copy.start()
        pending.append(copy)
        return copy

    def halves(count, half):
        first = (count + 1) // 2
        return pl.ds(0, first) if half == 0 else pl.ds(first, count - first)

    def gather_view(p, phase, at, half):
        first, second, third = ORDERS[p]
        buf = feats[p].at[core]
        if phase == 0:
            return buf.at[me[third], me[second], at, halves(COUNTS[p], half)]
        if phase == 1:
            return buf.at[me[third], at, pl.ds(2 * half, 2)]
        return buf.at[at, pl.ds(2 * half, 2)]

    def gather_copy(p, phase, number, at, half, target):
        view = gather_view(p, phase, at, half)
        return remote(view, view, ag_send.at[p, phase, number], ag_recv.at[p, phase, number], target)

    def pass_on(p, number, view):
        go(remote(view, view, sib_send.at[p, number], sib_recv.at[p, number], sibling))

    for p in range(3):
        first, second, third = ORDERS[p]
        feats[p][core, me[third], me[second], me[first]] = att[STARTS[p] : STARTS[p] + COUNTS[p]]

    def gather_start(p, phase):
        axis = ORDERS[p][phase]
        here = me[axis]
        found = [
            go(gather_copy(p, phase, 0, here, 0, nxt[axis])),
            go(gather_copy(p, phase, 1, here, 1, prv[axis])),
            go(gather_copy(p, phase, 2, here, 1, nxt[axis])),
            go(gather_copy(p, phase, 3, here, 0, prv[axis])),
        ]
        return found

    def gather_forward(p, phase, found):
        axis = ORDERS[p][phase]
        found[0].wait_recv()
        found.append(go(gather_copy(p, phase, 4, shifted(axis, 3), 0, nxt[axis])))
        found[1].wait_recv()
        found.append(go(gather_copy(p, phase, 5, shifted(axis, 1), 1, prv[axis])))

    for phase in range(3):
        founds = []
        for p in range(3):
            founds.append(gather_start(p, phase))
        if phase == 2:
            for p in range(3):
                pass_on(p, 0, feats[p].at[core, me[ORDERS[p][2]]])
        for p in range(3):
            gather_forward(p, phase, founds[p])
            if phase == 2:
                axis = ORDERS[p][2]
                pass_on(p, 1, gather_view(p, 2, shifted(axis, 3), 0))
                pass_on(p, 2, gather_view(p, 2, shifted(axis, 1), 1))
        if phase == 2:
            for load in loads:
                load.wait()
            scales[0] = scales_own[...].astype(jnp.float32)
            scales[1] = scales_other[...].astype(jnp.float32)
            diagonal = lax.broadcasted_iota(jnp.int32, (LANES, LANES), 0) == lax.broadcasted_iota(
                jnp.int32, (LANES, LANES), 1
            )

            def dequantize(step, carry):
                for k in range(8):
                    spot = step * 8 + k
                    where = table[0, spot]
                    row = scales[k % 2, pl.ds(where, 1), :]
                    spread = jnp.where(diagonal, jnp.broadcast_to(row, (LANES, LANES)), 0.0)
                    weights[spot] = jnp.dot(
                        spread.astype(jnp.bfloat16), tiles[k % 2, where],
                        preferred_element_type=jnp.float32,
                    ).astype(jnp.bfloat16)
                return carry

            lax.fori_loop(0, TILES // 8, dequantize, 0)
        for p in range(3):
            axis = ORDERS[p][phase]
            for number in (2, 3, 4, 5):
                founds[p][number].wait_recv()
                if phase == 2:
                    by, half = ((3, 1), (1, 0), (2, 0), (2, 1))[number - 2]
                    pass_on(p, number + 1, gather_view(p, 2, shifted(axis, by), half))

    for p in range(3):
        axis = ORDERS[p][2]
        for number in range(7):
            size = feats[p].at[core, 0] if number == 0 else feats[p].at[core, 0, pl.ds(0, 2)]
            remote(size, size, sib_send.at[p, number], sib_recv.at[p, number], sibling).wait_recv()

    for p in range(3):

        def multiply(step, carry, p=p):
            for k in range(8):
                spot = (STARTS[p] + step) * 8 + k
                part = table[1, spot]
                columns = []
                for j in range(2):
                    blocks = []
                    for x_lo in range(2):
                        for c in range(2):
                            for y in range(4):
                                at = {"x": part // 2 * 2 + x_lo, "y": y, "z": part % 2 * 2 + j}
                                first, second, third = ORDERS[p]
                                blocks.append(feats[p][c, at[third], at[second], at[first], step])
                    columns.append(jnp.concatenate(blocks, axis=0))
                left = jnp.concatenate(columns, axis=1)
                weight = weights[spot]
                none = jnp.zeros((64, LANES), jnp.bfloat16)
                if k < 4:
                    weight = jnp.concatenate([weight[:64], none, weight[64:], none], axis=0)
                else:
                    weight = jnp.concatenate([none, weight[:64], none, weight[64:]], axis=0)
                term = jnp.dot(left, weight, preferred_element_type=jnp.float32)
                link = table[2, spot]
                earlier = sums[jnp.maximum(link, 0)]
                sums[spot] = term + jnp.where(link >= 0, earlier, 0.0)
            return carry

        lax.fori_loop(0, COUNTS[p], multiply, 0)

    for p in range(3):

        def lay_out(step, carry, p=p):
            for x_lo in range(2):
                pair = []
                for k in range(2):
                    link = table[3, x_lo * 32 + (STARTS[p] + step) * 2 + k]
                    pair.append(jnp.where(link >= 0, sums[jnp.maximum(link, 0)], 0.0))
                for t in range(32):
                    at = {"x": t // 4 % 2 * 2 + x_lo, "y": t // 8, "z": t % 4}
                    first, second, third = ORDERS[p]
                    unit = jnp.concatenate([half[8 * t : 8 * t + 8] for half in pair], axis=0)
                    sends[p][at[first], at[second], at[third], step] = unit.astype(jnp.bfloat16)
            return carry

        lax.fori_loop(0, COUNTS[p], lay_out, 0)

    def scatter_at(p, phase, at):
        first, second, third = ORDERS[p]
        return [(), (me[first],), (me[first], me[second])][phase] + (at,)

    def part_of(phase, count, half):
        return halves(count, half) if phase == 2 else pl.ds(2 * half, 2)

    def scatter_view(p, phase, at, half):
        return sends[p].at[scatter_at(p, phase, at) + (part_of(phase, COUNTS[p], half),)]

    def scatter_start(p, phase):
        axis = ORDERS[p][phase]
        one_r, one_l, two_r, two_l = lands[p][phase]

        def copy(number, at, half, dst, target):
            return remote(
                scatter_view(p, phase, at, half), dst,
                rs_send.at[p, phase, number], rs_recv.at[p, phase, number], target,
            )

        def two(buf, half):
            return buf.at[part_of(phase, COUNTS[p], half)]

        right, left = shifted(axis, 1), shifted(axis, 3)
        far = shifted(axis, 2)
        return [
            go(copy(0, far, 0, one_r, nxt[axis])),
            go(copy(1, far, 1, one_l, prv[axis])),
            go(copy(2, right, 1, two(two_r, 1), nxt[axis])),
            go(copy(3, left, 0, two(two_l, 0), prv[axis])),
            copy(4, right, 0, two(two_r, 0), nxt[axis]),
            copy(5, left, 1, two(two_l, 1), prv[axis]),
        ]

    def add_in(p, phase, at, half, pieces):
        base = scatter_at(p, phase, at)
        offset = 2 if half == 1 else 0
        length = 4 if half is None else 2

        def added(spots, where):
            total = sends[p][spots].astype(jnp.float32)
            for piece in pieces:
                total = total + piece[where].astype(jnp.float32)
            return total.astype(jnp.bfloat16)

        if phase == 2:
            count = COUNTS[p]
            first = (count + 1) // 2
            begin, end = (0, count) if half is None else ((0, first) if half == 0 else (first, count))
            spots = base + (slice(begin, end),)
            sends[p][spots] = added(spots, (slice(0, end - begin),))
        elif phase == 1:
            for k in range(length):
                spots = base + (offset + k,)
                sends[p][spots] = added(spots, (k,))
        else:

            def step(k, carry):
                for m in range(4):
                    spots = base + (offset + k, m)
                    sends[p][spots] = added(spots, (k, m))
                return carry

            lax.fori_loop(0, length, step, 0)

    for phase in range(3):
        copies = [scatter_start(p, phase) for p in range(3)]
        for p in range(3):
            axis = ORDERS[p][phase]
            copies[p][0].wait_recv()
            add_in(p, phase, shifted(axis, 1), 0, [lands[p][phase][0]])
            go(copies[p][4])
            copies[p][1].wait_recv()
            add_in(p, phase, shifted(axis, 3), 1, [lands[p][phase][1]])
            go(copies[p][5])
        for p in range(3):
            axis = ORDERS[p][phase]
            for number in (2, 3, 4, 5):
                copies[p][number].wait_recv()
            if phase < 2:
                add_in(p, phase, me[axis], None, lands[p][phase][2:])
            else:
                base = scatter_at(p, phase, me[axis])
                for unit in range(COUNTS[p]):
                    total = sends[p][base + (unit,)].astype(jnp.float32)
                    for piece in lands[p][phase][2:]:
                        total = total + piece[unit].astype(jnp.float32)
                    column = (STARTS[p] + unit) * 2 * LANES
                    out[:, column : column + LANES] = total[:8].astype(jnp.bfloat16)
                    out[:, column + LANES : column + 2 * LANES] = total[8:].astype(jnp.bfloat16)

    for copy in pending:
        copy.wait_send()


def scratch_shapes():
    bf16 = jnp.bfloat16
    tail = (16, LANES)
    shapes = [pltpu.VMEM((2, 4, 4, 4, n) + tail, bf16) for n in COUNTS]
    shapes += [pltpu.VMEM((4, 4, 4, n) + tail, bf16) for n in COUNTS]
    for n in COUNTS:
        for lead in ((4, 4), (4,), ()):
            if lead:
                half = half_l = (2,) + lead[1:] + (n,)
            else:
                half, half_l = ((n + 1) // 2,), (n - (n + 1) // 2,)
            full = lead + (n,)
            for dims in (half, half_l, full, full):
                shapes.append(pltpu.VMEM(dims + tail, bf16))
    shapes += [
        pltpu.VMEM((2, TILES, LANES, LANES), bf16),
        pltpu.VMEM((2, TILES, LANES), jnp.float32),
        pltpu.VMEM((TILES, LANES, LANES), bf16),
        pltpu.VMEM((TILES, ROWS, LANES), jnp.float32),
        pltpu.SemaphoreType.DMA((2,)),
        pltpu.SemaphoreType.DMA((3, 3, 6)),
        pltpu.SemaphoreType.DMA((3, 3, 6)),
        pltpu.SemaphoreType.DMA((3, 7)),
        pltpu.SemaphoreType.DMA((3, 7)),
        pltpu.SemaphoreType.DMA((3, 3, 6)),
        pltpu.SemaphoreType.DMA((3, 3, 6)),
    ]
    return shapes


def body(queries, cache_keys, cache_values, lengths, old_tiles, old_scales, slot_tiles):
    grp, tp = lax.axis_index("grp"), lax.axis_index("tp")
    swap = [(0, 1), (1, 0), (2, 3), (3, 2)]
    other_tiles = lax.ppermute(old_tiles[0], "grp", swap)
    other_scales = lax.ppermute(old_scales[0], "grp", swap)
    table = tile_table(slot_tiles, grp, tp)
    group_rows = queries.shape[1]
    first_row = (grp * 32 + tp) // KV_HEADS * group_rows
    live_len = lax.dynamic_slice_in_dim(lengths, first_row, group_rows)
    att = attend_rows(queries[0], cache_keys[0], cache_values[0], live_len)
    vmem = pl.BlockSpec(memory_space=pltpu.VMEM)
    return pl.pallas_call(
        kernel,
        out_shape=jax.ShapeDtypeStruct((8, 4096), jnp.bfloat16),
        in_specs=[
            pl.BlockSpec(memory_space=pltpu.SMEM),
            vmem,
            pl.BlockSpec(memory_space=pl.ANY),
            pl.BlockSpec(memory_space=pl.ANY),
            vmem,
            vmem,
        ],
        out_specs=vmem,
        scratch_shapes=scratch_shapes(),
        compiler_params=pltpu.CompilerParams(
            collective_id=0, has_side_effects=True, vmem_limit_bytes=58 * 2**20
        ),
    )(table, att, old_tiles[0], other_tiles, old_scales[0], other_scales)


def solution(mesh):
    return jax.shard_map(
        body,
        mesh=mesh,
        in_specs=(
            P(("grp", "tp"), None, None),
            P(("grp", "tp"), None, None, None),
            P(("grp", "tp"), None, None, None),
            P(),
            P(("grp", "tp"), None, None, None),
            P(("grp", "tp"), None, None),
            P(),
        ),
        out_specs=P("tp", "grp"),
        check_vma=False,
    )
```

```python
import jax
import jax.numpy as jnp
from jax import lax
from jax.experimental import pallas as pl
from jax.experimental.pallas import tpu as pltpu
from jax.sharding import PartitionSpec as P

KV_HEADS = 8
HEAD_DIM = 128
HEADS = 16
LANES = 128
ORDERS = ("xyz", "yzx", "zxy")
COUNTS = (6, 5, 5)
STARTS = (0, 6, 11)
ROWS = 256
STAGE = 4
TILES = 128
MESH = pl.DeviceIdType.MESH


def tile_table(slot_tiles, grp, tp):
    core = grp % 2
    own = lax.dynamic_index_in_dim(slot_tiles, grp * 32 + tp, 0, keepdims=False)
    other = lax.dynamic_index_in_dim(
        slot_tiles, (grp + 1 - 2 * core) * 32 + tp, 0, keepdims=False
    )
    spot = lax.broadcasted_iota(jnp.int32, (TILES, TILES), 0)
    slot = lax.broadcasted_iota(jnp.int32, (TILES, TILES), 1)
    owner = ((spot // 2) % 2 * 2 + core) * 32 + spot // 4
    held = jnp.where(spot % 2 == 0, own[None], other[None])
    packed = slot * 128 + held % 128
    packed = jnp.sum(jnp.where(held // 128 == owner, packed, 0), axis=1)
    index = jnp.arange(TILES, dtype=jnp.int32)
    key = index // 2 % 2 * 32 + packed % 32
    before = (key[None] == key[:, None]) & (index[None] < index[:, None])
    previous = jnp.max(jnp.where(before, index[None], -1), axis=1)
    last = jnp.max(jnp.where(key[None] == index[:, None], index[None], -1), axis=1)
    return jnp.stack([packed // 128, packed % 128 // 32, previous, last])


def kernel(*refs):
    table, lengths, queries, keys, values, tiles_own, scales_own, out = refs[:8]
    scratch = list(refs[8:])
    feats = [scratch.pop(0) for _ in range(3)]
    sends = [scratch.pop(0) for _ in range(3)]
    lands = [[[scratch.pop(0) for _ in range(many)] for many in (4, 1, 1)] for _ in range(3)]
    tiles, scales, weights, sums = [scratch.pop(0) for _ in range(4)]
    key_buf, value_buf, att, scales_other = [scratch.pop(0) for _ in range(4)]
    kv_sem, swap_send, swap_recv = [scratch.pop(0) for _ in range(3)]
    load_sem, ag_send, ag_recv, sib_send, sib_recv, rs_send, rs_recv = scratch

    grp, tp = lax.axis_index("grp"), lax.axis_index("tp")
    core = lax.rem(grp, 2)
    me = {"x": lax.rem(lax.div(tp, 4), 2) * 2 + lax.div(grp, 2), "y": lax.div(tp, 8), "z": lax.rem(tp, 4)}

    def shifted(axis, by):
        return lax.rem(me[axis] + by, 4)

    def device(axis, by):
        at = dict(me)
        at[axis] = shifted(axis, by)
        return (
            lax.rem(at["x"], 2) * 2 + core,
            at["y"] * 8 + lax.div(at["x"], 2) * 4 + at["z"],
        )

    ring = {axis: [device(axis, by) for by in (1, 2, 3)] for axis in "xyz"}
    nxt = {axis: ring[axis][0] for axis in "xyz"}
    prv = {axis: ring[axis][2] for axis in "xyz"}
    sibling = (grp + 1 - 2 * core, tp)

    def kv_load(stage, slot):
        rows = pl.ds(stage * STAGE, STAGE)
        return [
            pltpu.make_async_copy(keys.at[rows], key_buf.at[slot], kv_sem.at[slot, 0]),
            pltpu.make_async_copy(values.at[rows], value_buf.at[slot], kv_sem.at[slot, 1]),
        ]

    for stage in range(2):
        for load in kv_load(stage, stage):
            load.start()
    loads = [pltpu.make_async_copy(tiles_own, tiles.at[0], load_sem.at[0])]
    for load in loads:
        load.start()

    barrier = pltpu.get_barrier_semaphore()
    for other in [*ring["x"], *ring["y"], *ring["z"], sibling]:
        pl.semaphore_signal(barrier, inc=1, device_id=other, device_id_type=MESH)

    def remote(src, dst, send, recv, target):
        return pltpu.make_async_remote_copy(
            src_ref=src, dst_ref=dst, send_sem=send, recv_sem=recv,
            device_id=target, device_id_type=MESH,
        )

    pending = []

    def go(copy):
        copy.start()
        pending.append(copy)
        return copy

    first_row = lax.div(grp * 32 + tp, KV_HEADS) * 16

    def attend(stage, carry):
        slot = lax.rem(stage, 2)
        for load in kv_load(stage, slot):
            load.wait()
        for k in range(STAGE):
            row = stage * STAGE + k
            scores = lax.dot_general(
                queries[row], key_buf[slot, k], (((1,), (1,)), ((), ())),
                preferred_element_type=jnp.float32,
            ) * HEAD_DIM ** (-0.5)
            inside = lax.broadcasted_iota(jnp.int32, scores.shape, 1) < lengths[first_row + row]
            scores = jnp.where(inside, scores, -1e30)
            row_max = jnp.max(scores, axis=1, keepdims=True)
            mass = jnp.where(inside, jnp.exp(scores - row_max), 0.0)
            share = 1.0 / jnp.sum(mass, axis=1, keepdims=True)
            mixed = jnp.dot(
                (mass * share).astype(jnp.bfloat16), value_buf[slot, k],
                preferred_element_type=jnp.float32,
            )
            att[:, pl.ds(row, 1), :] = mixed[:, None, :]

        @pl.when(stage < 16 // STAGE - 2)
        def _():
            for load in kv_load(stage + 2, slot):
                load.start()

        return carry

    lax.fori_loop(0, 16 // STAGE, attend, 0)
    pl.semaphore_wait(barrier, 10)
    def gather_view(p, phase, at, half):
        first, second, third = ORDERS[p]
        buf = feats[p].at[core]
        return buf.at[at, pl.ds(2 * half, 2)]

    def gather_direct(p, phase):
        first, second, third = ORDERS[p]
        axis = ORDERS[p][phase]
        buf = feats[p].at[core]
        view = buf.at[me[third], me[second], me[first]] if phase == 0 else buf.at[me[third], me[second]]
        return [
            go(remote(view, view, ag_send.at[p, phase, by], ag_recv.at[p, phase, by], ring[axis][by]))
            for by in range(3)
        ]

    def gather_copy(p, phase, number, at, half, target):
        view = gather_view(p, phase, at, half)
        return remote(view, view, ag_send.at[p, phase, number], ag_recv.at[p, phase, number], target)

    def pass_on(p, number, view):
        go(remote(view, view, sib_send.at[p, number], sib_recv.at[p, number], sibling))

    for p in range(3):
        first, second, third = ORDERS[p]
        feats[p][core, me[third], me[second], me[first]] = att[
            STARTS[p] : STARTS[p] + COUNTS[p]
        ].astype(jnp.bfloat16)

    def gather_start(p, phase):
        axis = ORDERS[p][phase]
        here = me[axis]
        found = [
            go(gather_copy(p, phase, 0, here, 0, nxt[axis])),
            go(gather_copy(p, phase, 1, here, 1, prv[axis])),
            go(gather_copy(p, phase, 2, here, 1, nxt[axis])),
            go(gather_copy(p, phase, 3, here, 0, prv[axis])),
        ]
        return found

    def gather_forward(p, phase, found):
        axis = ORDERS[p][phase]
        found[0].wait_recv()
        found.append(go(gather_copy(p, phase, 4, shifted(axis, 3), 0, nxt[axis])))
        found[1].wait_recv()
        found.append(go(gather_copy(p, phase, 5, shifted(axis, 1), 1, prv[axis])))

    for phase in range(2):
        founds = [gather_direct(p, phase) for p in range(3)]
        if phase == 0:
            swaps = [
                go(remote(tiles_own, tiles.at[1], swap_send.at[0], swap_recv.at[0], sibling)),
                go(remote(scales_own, scales_other, swap_send.at[1], swap_recv.at[1], sibling)),
            ]
        for found in founds:
            for copy in found:
                copy.wait_recv()
    phase = 2
    if phase == 2:
        founds = [gather_start(p, 2) for p in range(3)]
        for p in range(3):
            pass_on(p, 0, feats[p].at[core, me[ORDERS[p][2]]])
        for p in range(3):
            gather_forward(p, phase, founds[p])
            axis = ORDERS[p][2]
            pass_on(p, 1, gather_view(p, 2, shifted(axis, 3), 0))
            pass_on(p, 2, gather_view(p, 2, shifted(axis, 1), 1))
        if phase == 2:
            for load in loads:
                load.wait()
            for swap in swaps:
                swap.wait_recv()
            scales[0] = scales_own[...].astype(jnp.float32)
            scales[1] = scales_other[...].astype(jnp.float32)
            diagonal = lax.broadcasted_iota(jnp.int32, (LANES, LANES), 0) == lax.broadcasted_iota(
                jnp.int32, (LANES, LANES), 1
            )

            def dequantize(step, carry):
                for k in range(8):
                    spot = step * 8 + k
                    where = table[0, spot]
                    row = scales[k % 2, pl.ds(where, 1), :]
                    spread = jnp.where(diagonal, jnp.broadcast_to(row, (LANES, LANES)), 0.0)
                    weights[spot] = jnp.dot(
                        spread.astype(jnp.bfloat16), tiles[k % 2, where],
                        preferred_element_type=jnp.float32,
                    ).astype(jnp.bfloat16)
                return carry

            lax.fori_loop(0, TILES // 8, dequantize, 0)
        for p in range(3):
            axis = ORDERS[p][phase]
            for number in (2, 3, 4, 5):
                founds[p][number].wait_recv()
                if phase == 2:
                    by, half = ((3, 1), (1, 0), (2, 0), (2, 1))[number - 2]
                    pass_on(p, number + 1, gather_view(p, 2, shifted(axis, by), half))

    for p in range(3):
        axis = ORDERS[p][2]
        for number in range(7):
            size = feats[p].at[core, 0] if number == 0 else feats[p].at[core, 0, pl.ds(0, 2)]
            remote(size, size, sib_send.at[p, number], sib_recv.at[p, number], sibling).wait_recv()

    for p in range(3):

        def multiply(step, carry, p=p):
            for k in range(8):
                spot = (STARTS[p] + step) * 8 + k
                part = table[1, spot]
                columns = []
                for j in range(2):
                    blocks = []
                    for x_lo in range(2):
                        for c in range(2):
                            for y in range(4):
                                at = {"x": part // 2 * 2 + x_lo, "y": y, "z": part % 2 * 2 + j}
                                first, second, third = ORDERS[p]
                                blocks.append(feats[p][c, at[third], at[second], at[first], step])
                    columns.append(jnp.concatenate(blocks, axis=0))
                left = jnp.concatenate(columns, axis=1)
                weight = weights[spot]
                none = jnp.zeros((64, LANES), jnp.bfloat16)
                if k < 4:
                    weight = jnp.concatenate([weight[:64], none, weight[64:], none], axis=0)
                else:
                    weight = jnp.concatenate([none, weight[:64], none, weight[64:]], axis=0)
                term = jnp.dot(left, weight, preferred_element_type=jnp.float32)
                link = table[2, spot]
                earlier = sums[jnp.maximum(link, 0)]
                sums[spot] = term + jnp.where(link >= 0, earlier, 0.0)
            return carry

        lax.fori_loop(0, COUNTS[p], multiply, 0)

    def scatter_start(p):
        axis = ORDERS[p][0]
        one_r, one_l, two_r, two_l = lands[p][0]

        def half_of(buf, half):
            return buf.at[pl.ds(2 * half, 2)]

        def copy(number, at, half, dst, target):
            return remote(
                half_of(sends[p].at[at], half), dst,
                rs_send.at[p, 0, number], rs_recv.at[p, 0, number], target,
            )

        right, left = shifted(axis, 1), shifted(axis, 3)
        far = shifted(axis, 2)
        return [
            go(copy(0, far, 0, one_r, nxt[axis])),
            go(copy(1, far, 1, one_l, prv[axis])),
            go(copy(2, right, 1, half_of(two_r, 1), nxt[axis])),
            go(copy(3, left, 0, half_of(two_l, 0), prv[axis])),
            copy(4, right, 0, half_of(two_r, 0), nxt[axis]),
            copy(5, left, 1, half_of(two_l, 1), prv[axis]),
        ]

    def scatter_direct(p, phase):
        axis = ORDERS[p][phase]
        first, second, third = ORDERS[p]
        base = (me[first],) if phase == 1 else (me[first], me[second])
        return [
            go(
                remote(
                    sends[p].at[base + (shifted(axis, by + 1),)], lands[p][phase][0].at[by],
                    rs_send.at[p, phase, by], rs_recv.at[p, phase, by], ring[axis][by],
                )
            )
            for by in range(3)
        ]

    def add_in(p, at, half, pieces):
        offset = 2 if half == 1 else 0

        def step(k, carry):
            for m in range(4):
                total = sends[p][at, offset + k, m].astype(jnp.float32)
                for piece in pieces:
                    total = total + piece[k, m].astype(jnp.float32)
                sends[p][at, offset + k, m] = total.astype(jnp.bfloat16)
            return carry

        lax.fori_loop(0, 4 if half is None else 2, step, 0)

    copies = []
    for p in range(3):

        def lay_out(step, carry, p=p):
            for x_lo in range(2):
                pair = []
                for k in range(2):
                    link = table[3, x_lo * 32 + (STARTS[p] + step) * 2 + k]
                    pair.append(jnp.where(link >= 0, sums[jnp.maximum(link, 0)], 0.0))
                for t in range(32):
                    at = {"x": t // 4 % 2 * 2 + x_lo, "y": t // 8, "z": t % 4}
                    first, second, third = ORDERS[p]
                    unit = jnp.concatenate([half[8 * t : 8 * t + 8] for half in pair], axis=0)
                    sends[p][at[first], at[second], at[third], step] = unit.astype(jnp.bfloat16)
            return carry

        lax.fori_loop(0, COUNTS[p], lay_out, 0)
        copies.append(scatter_start(p))

    for p in range(3):
        axis = ORDERS[p][0]
        copies[p][0].wait_recv()
        add_in(p, shifted(axis, 1), 0, [lands[p][0][0]])
        go(copies[p][4])
        copies[p][1].wait_recv()
        add_in(p, shifted(axis, 3), 1, [lands[p][0][1]])
        go(copies[p][5])
    direct = []
    for p in range(3):
        for number in (2, 3, 4, 5):
            copies[p][number].wait_recv()
        add_in(p, me[ORDERS[p][0]], None, lands[p][0][2:])
        direct.append(scatter_direct(p, 1))
    last = []
    for p in range(3):
        for copy in direct[p]:
            copy.wait_recv()
        base = (me[ORDERS[p][0]], me[ORDERS[p][1]])
        for k in range(4):
            total = sends[p][base + (k,)].astype(jnp.float32)
            for by in range(3):
                total = total + lands[p][1][0][by, k].astype(jnp.float32)
            sends[p][base + (k,)] = total.astype(jnp.bfloat16)
        last.append(scatter_direct(p, 2))
    for p in range(3):
        for copy in last[p]:
            copy.wait_recv()
        base = (me[ORDERS[p][0]], me[ORDERS[p][1]], me[ORDERS[p][2]])
        for unit in range(COUNTS[p]):
            total = sends[p][base + (unit,)].astype(jnp.float32)
            for by in range(3):
                total = total + lands[p][2][0][by, unit].astype(jnp.float32)
            column = (STARTS[p] + unit) * 2 * LANES
            out[:, column : column + LANES] = total[:8].astype(jnp.bfloat16)
            out[:, column + LANES : column + 2 * LANES] = total[8:].astype(jnp.bfloat16)

    for copy in pending:
        copy.wait_send()


def scratch_shapes():
    bf16 = jnp.bfloat16
    tail = (16, LANES)
    shapes = [pltpu.VMEM((2, 4, 4, 4, n) + tail, bf16) for n in COUNTS]
    shapes += [pltpu.VMEM((4, 4, 4, n) + tail, bf16) for n in COUNTS]
    for n in COUNTS:
        shapes += [pltpu.VMEM((2, 4, n) + tail, bf16)] * 2 + [pltpu.VMEM((4, 4, n) + tail, bf16)] * 2
        shapes += [pltpu.VMEM((3, 4, n) + tail, bf16), pltpu.VMEM((3, n) + tail, bf16)]
    shapes += [
        pltpu.VMEM((2, TILES, LANES, LANES), bf16),
        pltpu.VMEM((2, TILES, LANES), jnp.float32),
        pltpu.VMEM((TILES, LANES, LANES), bf16),
        pltpu.VMEM((TILES, ROWS, LANES), jnp.float32),
        pltpu.VMEM((2, STAGE, 2048, LANES), bf16),
        pltpu.VMEM((2, STAGE, 2048, LANES), bf16),
        pltpu.VMEM((HEADS, 16, LANES), jnp.float32),
        pltpu.VMEM((TILES, LANES), bf16),
        pltpu.SemaphoreType.DMA((2, 2)),
        pltpu.SemaphoreType.DMA((2,)),
        pltpu.SemaphoreType.DMA((2,)),
        pltpu.SemaphoreType.DMA((1,)),
        pltpu.SemaphoreType.DMA((3, 3, 6)),
        pltpu.SemaphoreType.DMA((3, 3, 6)),
        pltpu.SemaphoreType.DMA((3, 7)),
        pltpu.SemaphoreType.DMA((3, 7)),
        pltpu.SemaphoreType.DMA((3, 3, 6)),
        pltpu.SemaphoreType.DMA((3, 3, 6)),
    ]
    return shapes


def body(queries, cache_keys, cache_values, lengths, old_tiles, old_scales, slot_tiles):
    grp, tp = lax.axis_index("grp"), lax.axis_index("tp")
    table = tile_table(slot_tiles, grp, tp)
    vmem = pl.BlockSpec(memory_space=pltpu.VMEM)
    return pl.pallas_call(
        kernel,
        out_shape=jax.ShapeDtypeStruct((8, 4096), jnp.bfloat16),
        in_specs=[
            pl.BlockSpec(memory_space=pltpu.SMEM),
            pl.BlockSpec(memory_space=pltpu.SMEM),
            vmem,
            pl.BlockSpec(memory_space=pl.ANY),
            pl.BlockSpec(memory_space=pl.ANY),
            pl.BlockSpec(memory_space=pl.ANY),
            vmem,
        ],
        out_specs=vmem,
        scratch_shapes=scratch_shapes(),
        compiler_params=pltpu.CompilerParams(
            collective_id=0, has_side_effects=True, vmem_limit_bytes=58 * 2**20
        ),
    )(
        table, lengths, queries.reshape(16, HEADS, HEAD_DIM), cache_keys[0], cache_values[0],
        old_tiles[0], old_scales[0],
    )


def solution(mesh):
    return jax.shard_map(
        body,
        mesh=mesh,
        in_specs=(
            P(("grp", "tp"), None, None),
            P(("grp", "tp"), None, None, None),
            P(("grp", "tp"), None, None, None),
            P(),
            P(("grp", "tp"), None, None, None),
            P(("grp", "tp"), None, None),
            P(),
        ),
        out_specs=P("tp", "grp"),
        check_vma=False,
    )
```

```python
import jax
import jax.numpy as jnp
from jax import lax
from jax.experimental import pallas as pl
from jax.experimental.pallas import tpu as pltpu
from jax.sharding import PartitionSpec as P

KV_HEADS = 8
HEAD_DIM = 128
HEADS = 16
LANES = 128
ORDERS = ("xyz", "yzx", "zxy")
COUNTS = (6, 5, 5)
STARTS = (0, 6, 11)
ROWS = 256
STAGE = 4
TILES = 128
MESH = pl.DeviceIdType.MESH


def tile_table(slot_tiles, grp, tp):
    core = grp % 2
    own = lax.dynamic_index_in_dim(slot_tiles, grp * 32 + tp, 0, keepdims=False)
    other = lax.dynamic_index_in_dim(
        slot_tiles, (grp + 1 - 2 * core) * 32 + tp, 0, keepdims=False
    )
    spot = lax.broadcasted_iota(jnp.int32, (TILES, TILES), 0)
    slot = lax.broadcasted_iota(jnp.int32, (TILES, TILES), 1)
    owner = ((spot // 2) % 2 * 2 + core) * 32 + spot // 4
    held = jnp.where(spot % 2 == 0, own[None], other[None])
    packed = slot * 128 + held % 128
    packed = jnp.sum(jnp.where(held // 128 == owner, packed, 0), axis=1)
    index = jnp.arange(TILES, dtype=jnp.int32)
    key = index // 2 % 2 * 32 + packed % 32
    before = (key[None] == key[:, None]) & (index[None] < index[:, None])
    previous = jnp.max(jnp.where(before, index[None], -1), axis=1)
    last = jnp.max(jnp.where(key[None] == index[:, None], index[None], -1), axis=1)
    return jnp.stack([packed // 128, packed % 128 // 32, previous, last])


def order_of(p, core):
    return ORDERS[(p + core) % 3]


def kernel(*refs):
    table, lengths, queries, keys, values, tiles_own, scales_own, out = refs[:8]
    scratch = list(refs[8:])
    feats = [scratch.pop(0) for _ in range(3)]
    sends = [scratch.pop(0) for _ in range(3)]
    lands = [[[scratch.pop(0) for _ in range(many)] for many in (4, 1, 1)] for _ in range(3)]
    tiles, scales, weights, sums = [scratch.pop(0) for _ in range(4)]
    key_buf, value_buf, att, scales_other, by_row = [scratch.pop(0) for _ in range(5)]
    kv_sem, swap_send, swap_recv = [scratch.pop(0) for _ in range(3)]
    load_sem, ag_send, ag_recv, sib_send, sib_recv, rs_send, rs_recv = scratch

    grp, tp = lax.axis_index("grp"), lax.axis_index("tp")
    core = lax.rem(grp, 2)
    me = {"x": lax.rem(lax.div(tp, 4), 2) * 2 + lax.div(grp, 2), "y": lax.div(tp, 8), "z": lax.rem(tp, 4)}

    def shifted(axis, by):
        return lax.rem(me[axis] + by, 4)

    def device(axis, by):
        at = dict(me)
        at[axis] = shifted(axis, by)
        return (
            lax.rem(at["x"], 2) * 2 + core,
            at["y"] * 8 + lax.div(at["x"], 2) * 4 + at["z"],
        )

    ring = {axis: [device(axis, by) for by in (1, 2, 3)] for axis in "xyz"}

    def either(a, b):
        return jnp.where(core == 0, a, b)

    spots, rings = [], []
    for p in range(3):
        mine = list(zip(order_of(p, 0), order_of(p, 1)))
        spots.append([either(me[a], me[b]) for a, b in mine])
        rings.append(
            [[tuple(map(either, ring[a][by], ring[b][by])) for by in range(3)] for a, b in mine]
        )

    def moved(p, phase, by):
        return lax.rem(spots[p][phase] + by, 4)

    sibling = (grp + 1 - 2 * core, tp)

    def kv_load(stage, slot):
        rows = pl.ds(stage * STAGE, STAGE)
        return [
            pltpu.make_async_copy(keys.at[rows], key_buf.at[slot], kv_sem.at[slot, 0]),
            pltpu.make_async_copy(values.at[rows], value_buf.at[slot], kv_sem.at[slot, 1]),
        ]

    for stage in range(2):
        for load in kv_load(stage, stage):
            load.start()
    loads = [pltpu.make_async_copy(tiles_own, tiles.at[0], load_sem.at[0])]

    barrier = pltpu.get_barrier_semaphore()
    for other in [*ring["x"], *ring["y"], *ring["z"], sibling]:
        pl.semaphore_signal(barrier, inc=1, device_id=other, device_id_type=MESH)

    def remote(src, dst, send, recv, target):
        return pltpu.make_async_remote_copy(
            src_ref=src, dst_ref=dst, send_sem=send, recv_sem=recv,
            device_id=target, device_id_type=MESH,
        )

    pending = []

    def go(copy):
        copy.start()
        pending.append(copy)
        return copy

    for h in range(HEADS):
        head = queries[:, h * HEAD_DIM : (h + 1) * HEAD_DIM].astype(jnp.float32)
        by_row[:, h : h + 1, :] = head[:, None, :]
    first_row = lax.div(grp * 32 + tp, KV_HEADS) * 16

    def attend(stage, carry):
        slot = lax.rem(stage, 2)
        for load in kv_load(stage, slot):
            load.wait()
        live, masses = [], []
        for k in range(STAGE):
            row = stage * STAGE + k
            scores = lax.dot_general(
                by_row[row].astype(jnp.bfloat16), key_buf[slot, k], (((1,), (1,)), ((), ())),
                preferred_element_type=jnp.float32,
            ) * HEAD_DIM ** (-0.5)
            live.append(scores)
        for k in range(STAGE):
            row = stage * STAGE + k
            inside = lax.broadcasted_iota(jnp.int32, live[k].shape, 1) < lengths[first_row + row]
            scores = jnp.where(inside, live[k], -1e30)
            row_max = jnp.max(scores, axis=1, keepdims=True)
            mass = jnp.where(inside, jnp.exp(scores - row_max), 0.0)
            share = 1.0 / jnp.sum(mass, axis=1, keepdims=True)
            masses.append((mass * share).astype(jnp.bfloat16))
        for k in range(STAGE):
            row = stage * STAGE + k
            mixed = jnp.dot(masses[k], value_buf[slot, k], preferred_element_type=jnp.float32)
            att[:, pl.ds(row, 1), :] = mixed[:, None, :]

        @pl.when(stage < 16 // STAGE - 2)
        def _():
            for load in kv_load(stage + 2, slot):
                load.start()

        return carry

    lax.fori_loop(0, 16 // STAGE, attend, 0)
    for load in loads:
        load.start()
    pl.semaphore_wait(barrier, 10)
    def gather_view(p, at, half):
        return feats[p].at[core, at, pl.ds(2 * half, 2)]

    def gather_direct(p, phase):
        first, second, third = spots[p]
        view = feats[p].at[core, third, second, first] if phase == 0 else feats[p].at[core, third, second]
        return [
            go(remote(view, view, ag_send.at[p, phase, by], ag_recv.at[p, phase, by], rings[p][phase][by]))
            for by in range(3)
        ]

    def gather_copy(p, number, at, half, target):
        view = gather_view(p, at, half)
        return go(remote(view, view, ag_send.at[p, 2, number], ag_recv.at[p, 2, number], target))

    def pass_on(p, number, view):
        go(remote(view, view, sib_send.at[p, number], sib_recv.at[p, number], sibling))

    def gather_start(p):
        here = spots[p][2]
        nxt, prv = rings[p][2][0], rings[p][2][2]
        return [
            gather_copy(p, 0, here, 0, nxt),
            gather_copy(p, 1, here, 1, prv),
            gather_copy(p, 2, here, 1, nxt),
            gather_copy(p, 3, here, 0, prv),
        ]

    def gather_forward(p, found):
        nxt, prv = rings[p][2][0], rings[p][2][2]
        found[0].wait_recv()
        found.append(gather_copy(p, 4, moved(p, 2, 3), 0, nxt))
        found[1].wait_recv()
        found.append(gather_copy(p, 5, moved(p, 2, 1), 1, prv))

    begun = []
    for p in range(3):
        first, second, third = spots[p]
        feats[p][core, third, second, first] = att[STARTS[p] : STARTS[p] + COUNTS[p]].astype(jnp.bfloat16)
        begun.append(gather_direct(p, 0))
    swaps = [
        go(remote(tiles_own, tiles.at[1], swap_send.at[0], swap_recv.at[0], sibling)),
        go(remote(scales_own, scales_other, swap_send.at[1], swap_recv.at[1], sibling)),
    ]
    across = []
    for p in range(3):
        for copy in begun[p]:
            copy.wait_recv()
        across.append(gather_direct(p, 1))
    founds = []
    for p in range(3):
        for copy in across[p]:
            copy.wait_recv()
        founds.append(gather_start(p))
        pass_on(p, 0, feats[p].at[core, spots[p][2]])
    for p in range(3):
        gather_forward(p, founds[p])
        pass_on(p, 1, gather_view(p, moved(p, 2, 3), 0))
        pass_on(p, 2, gather_view(p, moved(p, 2, 1), 1))
    for load in loads:
        load.wait()
    for swap in swaps:
        swap.wait_recv()
    scales[0] = scales_own[...].astype(jnp.float32)
    scales[1] = scales_other[...].astype(jnp.float32)
    diagonal = lax.broadcasted_iota(jnp.int32, (LANES, LANES), 0) == lax.broadcasted_iota(
        jnp.int32, (LANES, LANES), 1
    )

    def dequantize(step, carry):
        for k in range(8):
            spot = step * 8 + k
            where = table[0, spot]
            row = scales[k % 2, pl.ds(where, 1), :]
            spread = jnp.where(diagonal, jnp.broadcast_to(row, (LANES, LANES)), 0.0)
            weights[spot] = jnp.dot(
                spread.astype(jnp.bfloat16), tiles[k % 2, where],
                preferred_element_type=jnp.float32,
            ).astype(jnp.bfloat16)
        return carry

    lax.fori_loop(0, TILES // 8, dequantize, 0)
    for p in range(3):
        for number in (2, 3, 4, 5):
            founds[p][number].wait_recv()
            by, half = ((3, 1), (1, 0), (2, 0), (2, 1))[number - 2]
            pass_on(p, number + 1, gather_view(p, moved(p, 2, by), half))

    for p in range(3):
        for number in range(7):
            size = feats[p].at[core, 0] if number == 0 else feats[p].at[core, 0, pl.ds(0, 2)]
            remote(size, size, sib_send.at[p, number], sib_recv.at[p, number], sibling).wait_recv()

    for p in range(3):

        def multiply(step, carry, p=p):
            for k in range(8):
                spot = (STARTS[p] + step) * 8 + k
                part = table[1, spot]
                columns = []
                for j in range(2):
                    blocks = []
                    for x_lo in range(2):
                        for c in range(2):
                            for y in range(4):
                                at = {"x": part // 2 * 2 + x_lo, "y": y, "z": part % 2 * 2 + j}
                                first, second, third = order_of(p, c)
                                blocks.append(feats[p][c, at[third], at[second], at[first], step])
                    columns.append(jnp.concatenate(blocks, axis=0))
                left = jnp.concatenate(columns, axis=1)
                weight = weights[spot]
                none = jnp.zeros((64, LANES), jnp.bfloat16)
                if k < 4:
                    weight = jnp.concatenate([weight[:64], none, weight[64:], none], axis=0)
                else:
                    weight = jnp.concatenate([none, weight[:64], none, weight[64:]], axis=0)
                term = jnp.dot(left, weight, preferred_element_type=jnp.float32)
                link = table[2, spot]
                earlier = sums[jnp.maximum(link, 0)]
                sums[spot] = term + jnp.where(link >= 0, earlier, 0.0)
            return carry

        lax.fori_loop(0, COUNTS[p], multiply, 0)

    def scatter_start(p):
        nxt, prv = rings[p][0][0], rings[p][0][2]
        one_r, one_l, two_r, two_l = lands[p][0]

        def half_of(buf, half):
            return buf.at[pl.ds(2 * half, 2)]

        def copy(number, at, half, dst, target):
            return remote(
                half_of(sends[p].at[at], half), dst,
                rs_send.at[p, 0, number], rs_recv.at[p, 0, number], target,
            )

        right, far, left = (moved(p, 0, by) for by in (1, 2, 3))
        return [
            go(copy(0, far, 0, one_r, nxt)),
            go(copy(1, far, 1, one_l, prv)),
            go(copy(2, right, 1, half_of(two_r, 1), nxt)),
            go(copy(3, left, 0, half_of(two_l, 0), prv)),
            copy(4, right, 0, half_of(two_r, 0), nxt),
            copy(5, left, 1, half_of(two_l, 1), prv),
        ]

    def scatter_direct(p, phase):
        base = tuple(spots[p][:phase])
        return [
            go(
                remote(
                    sends[p].at[base + (moved(p, phase, by + 1),)], lands[p][phase][0].at[by],
                    rs_send.at[p, phase, by], rs_recv.at[p, phase, by], rings[p][phase][by],
                )
            )
            for by in range(3)
        ]

    def add_in(p, at, half, pieces):
        offset = 2 if half == 1 else 0

        def step(k, carry):
            for m in range(4):
                total = sends[p][at, offset + k, m].astype(jnp.float32)
                for piece in pieces:
                    total = total + piece[k, m].astype(jnp.float32)
                sends[p][at, offset + k, m] = total.astype(jnp.bfloat16)
            return carry

        lax.fori_loop(0, 4 if half is None else 2, step, 0)

    copies = []
    for p in range(3):

        def lay_out(step, carry, p=p):
            for x_lo in range(2):
                pair = []
                for k in range(2):
                    link = table[3, x_lo * 32 + (STARTS[p] + step) * 2 + k]
                    pair.append(jnp.where(link >= 0, sums[jnp.maximum(link, 0)], 0.0))
                for t in range(32):
                    at = {"x": t // 4 % 2 * 2 + x_lo, "y": t // 8, "z": t % 4}
                    zero, one = order_of(p, 0), order_of(p, 1)
                    first, second, third = (either(at[a], at[b]) for a, b in zip(zero, one))
                    unit = jnp.concatenate([half[8 * t : 8 * t + 8] for half in pair], axis=0)
                    sends[p][first, second, third, step] = unit.astype(jnp.bfloat16)
            return carry

        lax.fori_loop(0, COUNTS[p], lay_out, 0)
        copies.append(scatter_start(p))

    for p in range(3):
        copies[p][0].wait_recv()
        add_in(p, moved(p, 0, 1), 0, [lands[p][0][0]])
        go(copies[p][4])
        copies[p][1].wait_recv()
        add_in(p, moved(p, 0, 3), 1, [lands[p][0][1]])
        go(copies[p][5])
    direct = []
    for p in range(3):
        for number in (2, 3, 4, 5):
            copies[p][number].wait_recv()
        add_in(p, spots[p][0], None, lands[p][0][2:])
        direct.append(scatter_direct(p, 1))
    last = []
    for p in range(3):
        for copy in direct[p]:
            copy.wait_recv()
        base = tuple(spots[p][:2])
        for k in range(4):
            total = sends[p][base + (k,)].astype(jnp.float32)
            for by in range(3):
                total = total + lands[p][1][0][by, k].astype(jnp.float32)
            sends[p][base + (k,)] = total.astype(jnp.bfloat16)
        last.append(scatter_direct(p, 2))
    for p in range(3):
        for copy in last[p]:
            copy.wait_recv()
        base = tuple(spots[p])
        for unit in range(COUNTS[p]):
            total = sends[p][base + (unit,)].astype(jnp.float32)
            for by in range(3):
                total = total + lands[p][2][0][by, unit].astype(jnp.float32)
            column = (STARTS[p] + unit) * 2 * LANES
            out[:, column : column + LANES] = total[:8]
            out[:, column + LANES : column + 2 * LANES] = total[8:]

    for copy in pending:
        copy.wait_send()


def scratch_shapes():
    bf16 = jnp.bfloat16
    tail = (16, LANES)
    shapes = [pltpu.VMEM((2, 4, 4, 4, n) + tail, bf16) for n in COUNTS]
    shapes += [pltpu.VMEM((4, 4, 4, n) + tail, bf16) for n in COUNTS]
    for n in COUNTS:
        shapes += [pltpu.VMEM((2, 4, n) + tail, bf16)] * 2 + [pltpu.VMEM((4, 4, n) + tail, bf16)] * 2
        shapes += [pltpu.VMEM((3, 4, n) + tail, bf16), pltpu.VMEM((3, n) + tail, bf16)]
    shapes += [
        pltpu.VMEM((2, TILES, LANES, LANES), bf16),
        pltpu.VMEM((2, TILES, LANES), jnp.float32),
        pltpu.VMEM((TILES, LANES, LANES), bf16),
        pltpu.VMEM((TILES, ROWS, LANES), jnp.float32),
        pltpu.VMEM((2, STAGE, 2048, LANES), bf16),
        pltpu.VMEM((2, STAGE, 2048, LANES), bf16),
        pltpu.VMEM((HEADS, 16, LANES), jnp.float32),
        pltpu.VMEM((TILES, LANES), bf16),
        pltpu.VMEM((16, HEADS, LANES), jnp.float32),
        pltpu.SemaphoreType.DMA((2, 2)),
        pltpu.SemaphoreType.DMA((2,)),
        pltpu.SemaphoreType.DMA((2,)),
        pltpu.SemaphoreType.DMA((1,)),
        pltpu.SemaphoreType.DMA((3, 3, 6)),
        pltpu.SemaphoreType.DMA((3, 3, 6)),
        pltpu.SemaphoreType.DMA((3, 7)),
        pltpu.SemaphoreType.DMA((3, 7)),
        pltpu.SemaphoreType.DMA((3, 3, 6)),
        pltpu.SemaphoreType.DMA((3, 3, 6)),
    ]
    return shapes


def body(queries, cache_keys, cache_values, lengths, old_tiles, old_scales, slot_tiles):
    grp, tp = lax.axis_index("grp"), lax.axis_index("tp")
    table = tile_table(slot_tiles, grp, tp)
    vmem = pl.BlockSpec(memory_space=pltpu.VMEM)
    result = pl.pallas_call(
        kernel,
        out_shape=jax.ShapeDtypeStruct((8, 4096), jnp.float32),
        in_specs=[
            pl.BlockSpec(memory_space=pltpu.SMEM),
            pl.BlockSpec(memory_space=pltpu.SMEM),
            vmem,
            pl.BlockSpec(memory_space=pl.ANY),
            pl.BlockSpec(memory_space=pl.ANY),
            pl.BlockSpec(memory_space=pl.ANY),
            vmem,
        ],
        out_specs=vmem,
        scratch_shapes=scratch_shapes(),
        compiler_params=pltpu.CompilerParams(
            collective_id=0, has_side_effects=True, vmem_limit_bytes=58 * 2**20
        ),
    )(
        table, lengths, queries[0], cache_keys[0], cache_values[0],
        old_tiles[0], old_scales[0],
    )
    return result.astype(jnp.bfloat16)


def solution(mesh):
    return jax.shard_map(
        body,
        mesh=mesh,
        in_specs=(
            P(("grp", "tp"), None, None),
            P(("grp", "tp"), None, None, None),
            P(("grp", "tp"), None, None, None),
            P(),
            P(("grp", "tp"), None, None, None),
            P(("grp", "tp"), None, None),
            P(),
        ),
        out_specs=P("tp", "grp"),
        check_vma=False,
    )
```

```python
import jax
import jax.numpy as jnp
from jax import lax
from jax.experimental import pallas as pl
from jax.experimental.pallas import tpu as pltpu
from jax.sharding import PartitionSpec as P

KV_HEADS = 8
HEAD_DIM = 128
HEADS = 16
LANES = 128
ORDERS = ("xyz", "yzx", "zxy")
COUNTS = (6, 5, 5)
STARTS = (0, 6, 11)
ROWS = 256
STAGE = 4
TILES = 128
MESH = pl.DeviceIdType.MESH


def tile_table(own, other, core):
    shape = (TILES, TILES)
    spot = lax.broadcasted_iota(jnp.int32, shape, 0)
    lane = lax.broadcasted_iota(jnp.int32, shape, 1)

    def as_row(column):
        return jnp.sum(jnp.where(spot == lane, column, 0), axis=0, keepdims=True)

    x_lo = (spot >> 1) & 1
    held = jnp.where(
        (spot & 1) == 0, jnp.broadcast_to(own, shape), jnp.broadcast_to(other, shape)
    )
    match = (held >> 7) == (x_lo * 2 + core) * 32 + (spot >> 2)
    packed = jnp.max(jnp.where(match, lane * 128 + (held & 127), 0), axis=1, keepdims=True)
    packed = jnp.broadcast_to(packed, shape)
    key = x_lo * 32 + (packed & 31)
    key_row = jnp.broadcast_to(as_row(key), shape)
    before = (key_row == key) & (lane < spot)
    previous = jnp.max(jnp.where(before, lane, -1), axis=1, keepdims=True)
    last = jnp.max(jnp.where(key_row == spot, lane, -1), axis=1, keepdims=True)
    return [
        as_row(packed >> 7),
        as_row((packed >> 5) & 3),
        as_row(jnp.broadcast_to(previous, shape)),
        as_row(jnp.broadcast_to(last, shape)),
    ]


def order_of(p, core):
    return ORDERS[(p + core) % 3]


def kernel(*refs):
    slot_tiles, lengths, queries, keys, values, tiles_own, scales_own, out = refs[:8]
    scratch = list(refs[8:])
    feats = [scratch.pop(0) for _ in range(3)]
    sends = [scratch.pop(0) for _ in range(3)]
    lands = [[[scratch.pop(0) for _ in range(many)] for many in (4, 1, 1)] for _ in range(3)]
    tiles, scales, weights, sums = [scratch.pop(0) for _ in range(4)]
    key_buf, value_buf, att, scales_other, by_row = [scratch.pop(0) for _ in range(5)]
    table_vmem, table, table_sem = [scratch.pop(0) for _ in range(3)]
    kv_sem, swap_send, swap_recv = [scratch.pop(0) for _ in range(3)]
    load_sem, ag_send, ag_recv, sib_send, sib_recv, rs_send, rs_recv = scratch

    grp, tp = lax.axis_index("grp"), lax.axis_index("tp")
    core = lax.rem(grp, 2)
    me = {"x": lax.rem(lax.div(tp, 4), 2) * 2 + lax.div(grp, 2), "y": lax.div(tp, 8), "z": lax.rem(tp, 4)}

    def shifted(axis, by):
        return lax.rem(me[axis] + by, 4)

    def device(axis, by):
        at = dict(me)
        at[axis] = shifted(axis, by)
        return (
            lax.rem(at["x"], 2) * 2 + core,
            at["y"] * 8 + lax.div(at["x"], 2) * 4 + at["z"],
        )

    ring = {axis: [device(axis, by) for by in (1, 2, 3)] for axis in "xyz"}

    def either(a, b):
        return jnp.where(core == 0, a, b)

    spots, rings = [], []
    for p in range(3):
        mine = list(zip(order_of(p, 0), order_of(p, 1)))
        spots.append([either(me[a], me[b]) for a, b in mine])
        rings.append(
            [[tuple(map(either, ring[a][by], ring[b][by])) for by in range(3)] for a, b in mine]
        )

    def moved(p, phase, by):
        return lax.rem(spots[p][phase] + by, 4)

    sibling = (grp + 1 - 2 * core, tp)

    def kv_load(stage, slot):
        rows = pl.ds(stage * STAGE, STAGE)
        return [
            pltpu.make_async_copy(keys.at[rows], key_buf.at[slot], kv_sem.at[slot, 0]),
            pltpu.make_async_copy(values.at[rows], value_buf.at[slot], kv_sem.at[slot, 1]),
        ]

    for stage in range(2):
        for load in kv_load(stage, stage):
            load.start()
    loads = [pltpu.make_async_copy(tiles_own, tiles.at[0], load_sem.at[0])]

    barrier = pltpu.get_barrier_semaphore()
    for other in [*ring["x"], *ring["y"], *ring["z"], sibling]:
        pl.semaphore_signal(barrier, inc=1, device_id=other, device_id_type=MESH)

    def remote(src, dst, send, recv, target):
        return pltpu.make_async_remote_copy(
            src_ref=src, dst_ref=dst, send_sem=send, recv_sem=recv,
            device_id=target, device_id_type=MESH,
        )

    pending = []

    def go(copy):
        copy.start()
        pending.append(copy)
        return copy

    own = slot_tiles[pl.ds(grp * 32 + tp, 1), :]
    other = slot_tiles[pl.ds((grp + 1 - 2 * core) * 32 + tp, 1), :]
    for number, row in enumerate(tile_table(own, other, core)):
        table_vmem[number : number + 1, :] = row
    table_load = pltpu.make_async_copy(table_vmem, table, table_sem.at[0])
    table_load.start()

    for h in range(HEADS):
        head = queries[:, h * HEAD_DIM : (h + 1) * HEAD_DIM].astype(jnp.float32)
        by_row[:, h : h + 1, :] = head[:, None, :]
    first_row = lax.div(grp * 32 + tp, KV_HEADS) * 16

    def attend(stage, carry):
        slot = lax.rem(stage, 2)
        for load in kv_load(stage, slot):
            load.wait()
        live, masses = [], []
        for k in range(STAGE):
            row = stage * STAGE + k
            scores = lax.dot_general(
                by_row[row].astype(jnp.bfloat16), key_buf[slot, k], (((1,), (1,)), ((), ())),
                preferred_element_type=jnp.float32,
            ) * HEAD_DIM ** (-0.5)
            live.append(scores)
        for k in range(STAGE):
            row = stage * STAGE + k
            inside = lax.broadcasted_iota(jnp.int32, live[k].shape, 1) < lengths[first_row + row]
            scores = jnp.where(inside, live[k], -1e30)
            row_max = jnp.max(scores, axis=1, keepdims=True)
            mass = jnp.where(inside, jnp.exp(scores - row_max), 0.0)
            share = 1.0 / jnp.sum(mass, axis=1, keepdims=True)
            masses.append((mass * share).astype(jnp.bfloat16))
        for k in range(STAGE):
            row = stage * STAGE + k
            mixed = jnp.dot(masses[k], value_buf[slot, k], preferred_element_type=jnp.float32)
            att[:, pl.ds(row, 1), :] = mixed[:, None, :]

        @pl.when(stage < 16 // STAGE - 2)
        def _():
            for load in kv_load(stage + 2, slot):
                load.start()

        return carry

    lax.fori_loop(0, 16 // STAGE, attend, 0)
    for load in loads:
        load.start()
    pl.semaphore_wait(barrier, 10)
    def gather_view(p, at, half):
        return feats[p].at[core, at, pl.ds(2 * half, 2)]

    def gather_direct(p, phase):
        first, second, third = spots[p]
        view = feats[p].at[core, third, second, first] if phase == 0 else feats[p].at[core, third, second]
        return [
            go(remote(view, view, ag_send.at[p, phase, by], ag_recv.at[p, phase, by], rings[p][phase][by]))
            for by in range(3)
        ]

    def gather_copy(p, number, at, half, target):
        view = gather_view(p, at, half)
        return go(remote(view, view, ag_send.at[p, 2, number], ag_recv.at[p, 2, number], target))

    def pass_on(p, number, view):
        go(remote(view, view, sib_send.at[p, number], sib_recv.at[p, number], sibling))

    def gather_start(p):
        here = spots[p][2]
        nxt, prv = rings[p][2][0], rings[p][2][2]
        return [
            gather_copy(p, 0, here, 0, nxt),
            gather_copy(p, 1, here, 1, prv),
            gather_copy(p, 2, here, 1, nxt),
            gather_copy(p, 3, here, 0, prv),
        ]

    def gather_forward(p, found):
        nxt, prv = rings[p][2][0], rings[p][2][2]
        found[0].wait_recv()
        found.append(gather_copy(p, 4, moved(p, 2, 3), 0, nxt))
        found[1].wait_recv()
        found.append(gather_copy(p, 5, moved(p, 2, 1), 1, prv))

    begun = []
    for p in range(3):
        first, second, third = spots[p]
        feats[p][core, third, second, first] = att[STARTS[p] : STARTS[p] + COUNTS[p]].astype(jnp.bfloat16)
        begun.append(gather_direct(p, 0))
    swaps = [
        go(remote(tiles_own, tiles.at[1], swap_send.at[0], swap_recv.at[0], sibling)),
        go(remote(scales_own, scales_other, swap_send.at[1], swap_recv.at[1], sibling)),
    ]
    across = []
    for p in range(3):
        for copy in begun[p]:
            copy.wait_recv()
        across.append(gather_direct(p, 1))
    founds = []
    for p in range(3):
        for copy in across[p]:
            copy.wait_recv()
        founds.append(gather_start(p))
        pass_on(p, 0, feats[p].at[core, spots[p][2]])
    for p in range(3):
        gather_forward(p, founds[p])
        pass_on(p, 1, gather_view(p, moved(p, 2, 3), 0))
        pass_on(p, 2, gather_view(p, moved(p, 2, 1), 1))
    for load in loads:
        load.wait()
    table_load.wait()
    for swap in swaps:
        swap.wait_recv()
    scales[0] = scales_own[...].astype(jnp.float32)
    scales[1] = scales_other[...].astype(jnp.float32)
    diagonal = lax.broadcasted_iota(jnp.int32, (LANES, LANES), 0) == lax.broadcasted_iota(
        jnp.int32, (LANES, LANES), 1
    )

    def dequantize(step, carry):
        for k in range(8):
            spot = step * 8 + k
            where = table[0, spot]
            row = scales[k % 2, pl.ds(where, 1), :]
            spread = jnp.where(diagonal, jnp.broadcast_to(row, (LANES, LANES)), 0.0)
            weights[spot] = jnp.dot(
                spread.astype(jnp.bfloat16), tiles[k % 2, where],
                preferred_element_type=jnp.float32,
            ).astype(jnp.bfloat16)
        return carry

    lax.fori_loop(0, TILES // 8, dequantize, 0)
    for p in range(3):
        for number in (2, 3, 4, 5):
            founds[p][number].wait_recv()
            by, half = ((3, 1), (1, 0), (2, 0), (2, 1))[number - 2]
            pass_on(p, number + 1, gather_view(p, moved(p, 2, by), half))

    for p in range(3):
        for number in range(7):
            size = feats[p].at[core, 0] if number == 0 else feats[p].at[core, 0, pl.ds(0, 2)]
            remote(size, size, sib_send.at[p, number], sib_recv.at[p, number], sibling).wait_recv()

        def multiply(step, carry, p=p):
            for k in range(8):
                spot = (STARTS[p] + step) * 8 + k
                part = table[1, spot]
                columns = []
                for j in range(2):
                    blocks = []
                    for x_lo in range(2):
                        for c in range(2):
                            for y in range(4):
                                at = {"x": part // 2 * 2 + x_lo, "y": y, "z": part % 2 * 2 + j}
                                first, second, third = order_of(p, c)
                                blocks.append(feats[p][c, at[third], at[second], at[first], step])
                    columns.append(jnp.concatenate(blocks, axis=0))
                left = jnp.concatenate(columns, axis=1)
                weight = weights[spot]
                none = jnp.zeros((64, LANES), jnp.bfloat16)
                if k < 4:
                    weight = jnp.concatenate([weight[:64], none, weight[64:], none], axis=0)
                else:
                    weight = jnp.concatenate([none, weight[:64], none, weight[64:]], axis=0)
                term = jnp.dot(left, weight, preferred_element_type=jnp.float32)
                link = table[2, spot]
                earlier = sums[jnp.maximum(link, 0)]
                sums[spot] = term + jnp.where(link >= 0, earlier, 0.0)
            return carry

        lax.fori_loop(0, COUNTS[p], multiply, 0)

    def scatter_start(p):
        nxt, prv = rings[p][0][0], rings[p][0][2]
        one_r, one_l, two_r, two_l = lands[p][0]

        def half_of(buf, half):
            return buf.at[pl.ds(2 * half, 2)]

        def copy(number, at, half, dst, target):
            return remote(
                half_of(sends[p].at[at], half), dst,
                rs_send.at[p, 0, number], rs_recv.at[p, 0, number], target,
            )

        right, far, left = (moved(p, 0, by) for by in (1, 2, 3))
        return [
            go(copy(0, far, 0, one_r, nxt)),
            go(copy(1, far, 1, one_l, prv)),
            go(copy(2, right, 1, half_of(two_r, 1), nxt)),
            go(copy(3, left, 0, half_of(two_l, 0), prv)),
            copy(4, right, 0, half_of(two_r, 0), nxt),
            copy(5, left, 1, half_of(two_l, 1), prv),
        ]

    def scatter_direct(p, phase):
        base = tuple(spots[p][:phase])
        return [
            go(
                remote(
                    sends[p].at[base + (moved(p, phase, by + 1),)], lands[p][phase][0].at[by],
                    rs_send.at[p, phase, by], rs_recv.at[p, phase, by], rings[p][phase][by],
                )
            )
            for by in range(3)
        ]

    def add_in(p, at, half, pieces):
        offset = 2 if half == 1 else 0

        def step(k, carry):
            totals = []
            for m in range(4):
                total = sends[p][at, offset + k, m].astype(jnp.float32)
                for piece in pieces:
                    total = total + piece[k, m].astype(jnp.float32)
                totals.append(total.astype(jnp.bfloat16))
            for m in range(4):
                sends[p][at, offset + k, m] = totals[m]
            return carry

        lax.fori_loop(0, 4 if half is None else 2, step, 0)

    copies = []
    for p in range(3):

        def lay_out(step, carry, p=p):
            for x_lo in range(2):
                pair = []
                for k in range(2):
                    link = table[3, x_lo * 32 + (STARTS[p] + step) * 2 + k]
                    pair.append(jnp.where(link >= 0, sums[jnp.maximum(link, 0)], 0.0))
                for t in range(32):
                    at = {"x": t // 4 % 2 * 2 + x_lo, "y": t // 8, "z": t % 4}
                    zero, one = order_of(p, 0), order_of(p, 1)
                    first, second, third = (either(at[a], at[b]) for a, b in zip(zero, one))
                    unit = jnp.concatenate([half[8 * t : 8 * t + 8] for half in pair], axis=0)
                    sends[p][first, second, third, step] = unit.astype(jnp.bfloat16)
            return carry

        lax.fori_loop(0, COUNTS[p], lay_out, 0)
        copies.append(scatter_start(p))

    for p in range(3):
        copies[p][0].wait_recv()
        add_in(p, moved(p, 0, 1), 0, [lands[p][0][0]])
        go(copies[p][4])
        copies[p][1].wait_recv()
        add_in(p, moved(p, 0, 3), 1, [lands[p][0][1]])
        go(copies[p][5])
    direct = []
    for p in range(3):
        for number in (2, 3, 4, 5):
            copies[p][number].wait_recv()
        add_in(p, spots[p][0], None, lands[p][0][2:])
        direct.append(scatter_direct(p, 1))
    last = []
    for p in range(3):
        for copy in direct[p]:
            copy.wait_recv()
        base = tuple(spots[p][:2])
        totals = []
        for k in range(4):
            total = sends[p][base + (k,)].astype(jnp.float32)
            for by in range(3):
                total = total + lands[p][1][0][by, k].astype(jnp.float32)
            totals.append(total.astype(jnp.bfloat16))
        for k in range(4):
            sends[p][base + (k,)] = totals[k]
        last.append(scatter_direct(p, 2))
    for p in range(3):
        for copy in last[p]:
            copy.wait_recv()
        base = tuple(spots[p])
        for unit in range(COUNTS[p]):
            total = sends[p][base + (unit,)].astype(jnp.float32)
            for by in range(3):
                total = total + lands[p][2][0][by, unit].astype(jnp.float32)
            column = (STARTS[p] + unit) * 2 * LANES
            out[:, column : column + LANES] = total[:8].astype(jnp.bfloat16)
            out[:, column + LANES : column + 2 * LANES] = total[8:].astype(jnp.bfloat16)

    for copy in pending:
        copy.wait_send()


def scratch_shapes():
    bf16 = jnp.bfloat16
    tail = (16, LANES)
    shapes = [pltpu.VMEM((2, 4, 4, 4, n) + tail, bf16) for n in COUNTS]
    shapes += [pltpu.VMEM((4, 4, 4, n) + tail, bf16) for n in COUNTS]
    for n in COUNTS:
        shapes += [pltpu.VMEM((2, 4, n) + tail, bf16)] * 2 + [pltpu.VMEM((4, 4, n) + tail, bf16)] * 2
        shapes += [pltpu.VMEM((3, 4, n) + tail, bf16), pltpu.VMEM((3, n) + tail, bf16)]
    shapes += [
        pltpu.VMEM((2, TILES, LANES, LANES), bf16),
        pltpu.VMEM((2, TILES, LANES), jnp.float32),
        pltpu.VMEM((TILES, LANES, LANES), bf16),
        pltpu.VMEM((TILES, ROWS, LANES), jnp.float32),
        pltpu.VMEM((2, STAGE, 2048, LANES), bf16),
        pltpu.VMEM((2, STAGE, 2048, LANES), bf16),
        pltpu.VMEM((HEADS, 16, LANES), jnp.float32),
        pltpu.VMEM((TILES, LANES), bf16),
        pltpu.VMEM((16, HEADS, LANES), jnp.float32),
        pltpu.VMEM((8, TILES), jnp.int32),
        pltpu.SMEM((8, TILES), jnp.int32),
        pltpu.SemaphoreType.DMA((1,)),
        pltpu.SemaphoreType.DMA((2, 2)),
        pltpu.SemaphoreType.DMA((2,)),
        pltpu.SemaphoreType.DMA((2,)),
        pltpu.SemaphoreType.DMA((1,)),
        pltpu.SemaphoreType.DMA((3, 3, 6)),
        pltpu.SemaphoreType.DMA((3, 3, 6)),
        pltpu.SemaphoreType.DMA((3, 7)),
        pltpu.SemaphoreType.DMA((3, 7)),
        pltpu.SemaphoreType.DMA((3, 3, 6)),
        pltpu.SemaphoreType.DMA((3, 3, 6)),
    ]
    return shapes


def body(queries, cache_keys, cache_values, lengths, old_tiles, old_scales, slot_tiles):
    vmem = pl.BlockSpec(memory_space=pltpu.VMEM)
    return pl.pallas_call(
        kernel,
        out_shape=jax.ShapeDtypeStruct((8, 4096), jnp.bfloat16),
        in_specs=[
            vmem,
            pl.BlockSpec(memory_space=pltpu.SMEM),
            vmem,
            pl.BlockSpec(memory_space=pl.ANY),
            pl.BlockSpec(memory_space=pl.ANY),
            pl.BlockSpec(memory_space=pl.ANY),
            vmem,
        ],
        out_specs=vmem,
        scratch_shapes=scratch_shapes(),
        compiler_params=pltpu.CompilerParams(
            collective_id=0, has_side_effects=True, vmem_limit_bytes=58 * 2**20
        ),
    )(
        slot_tiles, lengths, queries[0], cache_keys[0], cache_values[0],
        old_tiles[0], old_scales[0],
    )


def solution(mesh):
    return jax.shard_map(
        body,
        mesh=mesh,
        in_specs=(
            P(("grp", "tp"), None, None),
            P(("grp", "tp"), None, None, None),
            P(("grp", "tp"), None, None, None),
            P(),
            P(("grp", "tp"), None, None, None),
            P(("grp", "tp"), None, None),
            P(),
        ),
        out_specs=P("tp", "grp"),
        check_vma=False,
    )
```

```python
import jax
import jax.numpy as jnp
from jax import lax
from jax.experimental import pallas as pl
from jax.experimental.pallas import tpu as pltpu
from jax.sharding import PartitionSpec as P

KV_HEADS = 8
HEAD_DIM = 128
HEADS = 16
LANES = 128
ORDERS = ("xyz", "yzx", "zxy")
COUNTS = (6, 5, 5)
STARTS = (0, 6, 11)
ROWS = 256
STAGE = 4
TILES = 128
MESH = pl.DeviceIdType.MESH


def tile_table(own, other, core):
    shape = (TILES, TILES)
    spot = lax.broadcasted_iota(jnp.int32, shape, 0)
    lane = lax.broadcasted_iota(jnp.int32, shape, 1)

    def as_row(column):
        return jnp.sum(jnp.where(spot == lane, column, 0), axis=0, keepdims=True)

    x_lo = (spot >> 1) & 1
    held = jnp.where(
        (spot & 1) == 0, jnp.broadcast_to(own, shape), jnp.broadcast_to(other, shape)
    )
    match = (held >> 7) == (x_lo * 2 + core) * 32 + (spot >> 2)
    packed = jnp.max(jnp.where(match, lane * 128 + (held & 127), 0), axis=1, keepdims=True)
    packed = jnp.broadcast_to(packed, shape)
    key = x_lo * 32 + (packed & 31)
    key_row = jnp.broadcast_to(as_row(key), shape)
    before = (key_row == key) & (lane < spot)
    previous = jnp.max(jnp.where(before, lane, -1), axis=1, keepdims=True)
    last = jnp.max(jnp.where(key_row == spot, lane, -1), axis=1, keepdims=True)
    return [
        as_row(packed >> 7),
        as_row((packed >> 5) & 3),
        as_row(jnp.broadcast_to(previous, shape)),
        as_row(jnp.broadcast_to(last, shape)),
    ]


def order_of(p, core):
    return ORDERS[(p + core) % 3]


def kernel(*refs):
    slot_tiles, lengths, queries, keys, values, tiles_own, scales_own, out = refs[:8]
    scratch = list(refs[8:])
    feats = [scratch.pop(0) for _ in range(3)]
    sends = [scratch.pop(0) for _ in range(3)]
    lands = [[[scratch.pop(0) for _ in range(many)] for many in (4, 1, 1)] for _ in range(3)]
    tiles, scales, weights, sums = [scratch.pop(0) for _ in range(4)]
    key_buf, value_buf, att, scales_other, by_row = [scratch.pop(0) for _ in range(5)]
    table_vmem, table, table_sem = [scratch.pop(0) for _ in range(3)]
    kv_sem, swap_send, swap_recv = [scratch.pop(0) for _ in range(3)]
    load_sem, ag_send, ag_recv, sib_send, sib_recv, rs_send, rs_recv = scratch

    grp, tp = lax.axis_index("grp"), lax.axis_index("tp")
    core = lax.rem(grp, 2)
    me = {"x": lax.rem(lax.div(tp, 4), 2) * 2 + lax.div(grp, 2), "y": lax.div(tp, 8), "z": lax.rem(tp, 4)}

    def shifted(axis, by):
        return lax.rem(me[axis] + by, 4)

    def device(axis, by):
        at = dict(me)
        at[axis] = shifted(axis, by)
        return (
            lax.rem(at["x"], 2) * 2 + core,
            at["y"] * 8 + lax.div(at["x"], 2) * 4 + at["z"],
        )

    ring = {axis: [device(axis, by) for by in (1, 2, 3)] for axis in "xyz"}

    def either(a, b):
        return jnp.where(core == 0, a, b)

    spots, rings = [], []
    for p in range(3):
        mine = list(zip(order_of(p, 0), order_of(p, 1)))
        spots.append([either(me[a], me[b]) for a, b in mine])
        rings.append(
            [[tuple(map(either, ring[a][by], ring[b][by])) for by in range(3)] for a, b in mine]
        )

    def moved(p, phase, by):
        return lax.rem(spots[p][phase] + by, 4)

    sibling = (grp + 1 - 2 * core, tp)

    def kv_load(stage, slot):
        rows = pl.ds(stage * STAGE, STAGE)
        return [
            pltpu.make_async_copy(keys.at[rows], key_buf.at[slot], kv_sem.at[slot, 0]),
            pltpu.make_async_copy(values.at[rows], value_buf.at[slot], kv_sem.at[slot, 1]),
        ]

    for stage in range(2):
        for load in kv_load(stage, stage):
            load.start()
    loads = [pltpu.make_async_copy(tiles_own, tiles.at[0], load_sem.at[0])]

    barrier = pltpu.get_barrier_semaphore()
    for other in [*ring["x"], *ring["y"], *ring["z"], sibling]:
        pl.semaphore_signal(barrier, inc=1, device_id=other, device_id_type=MESH)

    def remote(src, dst, send, recv, target):
        return pltpu.make_async_remote_copy(
            src_ref=src, dst_ref=dst, send_sem=send, recv_sem=recv,
            device_id=target, device_id_type=MESH,
        )

    pending = []

    def go(copy):
        copy.start()
        pending.append(copy)
        return copy

    own = slot_tiles[pl.ds(grp * 32 + tp, 1), :]
    other = slot_tiles[pl.ds((grp + 1 - 2 * core) * 32 + tp, 1), :]
    for number, row in enumerate(tile_table(own, other, core)):
        table_vmem[number : number + 1, :] = row
    table_load = pltpu.make_async_copy(table_vmem, table, table_sem.at[0])
    table_load.start()

    for h in range(HEADS):
        head = queries[:, h * HEAD_DIM : (h + 1) * HEAD_DIM].astype(jnp.float32)
        by_row[:, h : h + 1, :] = head[:, None, :]
    first_row = lax.div(grp * 32 + tp, KV_HEADS) * 16

    def attend(stage, carry):
        slot = lax.rem(stage, 2)
        for load in kv_load(stage, slot):
            load.wait()
        live, masses = [], []
        for k in range(STAGE):
            row = stage * STAGE + k
            scores = lax.dot_general(
                by_row[row].astype(jnp.bfloat16), key_buf[slot, k], (((1,), (1,)), ((), ())),
                preferred_element_type=jnp.float32,
            ) * HEAD_DIM ** (-0.5)
            live.append(scores)
        for k in range(STAGE):
            row = stage * STAGE + k
            inside = lax.broadcasted_iota(jnp.int32, live[k].shape, 1) < lengths[first_row + row]
            scores = jnp.where(inside, live[k], -1e30)
            row_max = jnp.max(scores, axis=1, keepdims=True)
            mass = jnp.where(inside, jnp.exp(scores - row_max), 0.0)
            share = 1.0 / jnp.sum(mass, axis=1, keepdims=True)
            masses.append((mass * share).astype(jnp.bfloat16))
        for k in range(STAGE):
            row = stage * STAGE + k
            mixed = jnp.dot(masses[k], value_buf[slot, k], preferred_element_type=jnp.float32)
            att[:, pl.ds(row, 1), :] = mixed[:, None, :]

        @pl.when(stage < 16 // STAGE - 2)
        def _():
            for load in kv_load(stage + 2, slot):
                load.start()

        return carry

    lax.fori_loop(0, 16 // STAGE, attend, 0)
    for load in loads:
        load.start()
    pl.semaphore_wait(barrier, 10)
    def gather_view(p, at, half):
        return feats[p].at[core, at, pl.ds(2 * half, 2)]

    def gather_direct(p, phase):
        first, second, third = spots[p]
        view = feats[p].at[core, third, second, first] if phase == 0 else feats[p].at[core, third, second]
        return [
            go(remote(view, view, ag_send.at[p, phase, by], ag_recv.at[p, phase, by], rings[p][phase][by]))
            for by in range(3)
        ]

    def gather_copy(p, number, at, half, target):
        view = gather_view(p, at, half)
        return go(remote(view, view, ag_send.at[p, 2, number], ag_recv.at[p, 2, number], target))

    def pass_on(p, number, view):
        go(remote(view, view, sib_send.at[p, number], sib_recv.at[p, number], sibling))

    def gather_start(p):
        here = spots[p][2]
        nxt, prv = rings[p][2][0], rings[p][2][2]
        return [
            gather_copy(p, 0, here, 0, nxt),
            gather_copy(p, 1, here, 1, prv),
            gather_copy(p, 2, here, 1, nxt),
            gather_copy(p, 3, here, 0, prv),
        ]

    def gather_forward(p, found):
        nxt, prv = rings[p][2][0], rings[p][2][2]
        found[0].wait_recv()
        found.append(gather_copy(p, 4, moved(p, 2, 3), 0, nxt))
        found[1].wait_recv()
        found.append(gather_copy(p, 5, moved(p, 2, 1), 1, prv))

    begun = []
    for p in range(3):
        first, second, third = spots[p]
        feats[p][core, third, second, first] = att[STARTS[p] : STARTS[p] + COUNTS[p]].astype(jnp.bfloat16)
        begun.append(gather_direct(p, 0))
    swaps = [
        go(remote(tiles_own, tiles.at[1], swap_send.at[0], swap_recv.at[0], sibling)),
        go(remote(scales_own, scales_other, swap_send.at[1], swap_recv.at[1], sibling)),
    ]
    across = []
    for p in range(3):
        for copy in begun[p]:
            copy.wait_recv()
        across.append(gather_direct(p, 1))
    founds = []
    for p in range(3):
        for copy in across[p]:
            copy.wait_recv()
        founds.append(gather_start(p))
        pass_on(p, 0, feats[p].at[core, spots[p][2]])
    for p in range(3):
        gather_forward(p, founds[p])
        pass_on(p, 1, gather_view(p, moved(p, 2, 3), 0))
        pass_on(p, 2, gather_view(p, moved(p, 2, 1), 1))
    for load in loads:
        load.wait()
    table_load.wait()
    for swap in swaps:
        swap.wait_recv()
    scales[0] = scales_own[...].astype(jnp.float32)
    scales[1] = scales_other[...].astype(jnp.float32)
    diagonal = lax.broadcasted_iota(jnp.int32, (LANES, LANES), 0) == lax.broadcasted_iota(
        jnp.int32, (LANES, LANES), 1
    )

    def dequantize(step, carry):
        for k in range(8):
            spot = step * 8 + k
            where = table[0, spot]
            row = scales[k % 2, pl.ds(where, 1), :]
            spread = jnp.where(diagonal, jnp.broadcast_to(row, (LANES, LANES)), 0.0)
            weights[spot] = jnp.dot(
                spread.astype(jnp.bfloat16), tiles[k % 2, where],
                preferred_element_type=jnp.float32,
            ).astype(jnp.bfloat16)
        return carry

    lax.fori_loop(0, TILES // 8, dequantize, 0)
    for p in range(3):
        for number in (2, 3, 4, 5):
            founds[p][number].wait_recv()
            by, half = ((3, 1), (1, 0), (2, 0), (2, 1))[number - 2]
            pass_on(p, number + 1, gather_view(p, moved(p, 2, by), half))

    for p in range(3):
        for number in range(7):
            size = feats[p].at[core, 0] if number == 0 else feats[p].at[core, 0, pl.ds(0, 2)]
            remote(size, size, sib_send.at[p, number], sib_recv.at[p, number], sibling).wait_recv()

        def multiply(step, carry, p=p):
            for k in range(8):
                spot = (STARTS[p] + step) * 8 + k
                part = table[1, spot]
                columns = []
                for j in range(2):
                    found = []
                    for c in range(2):
                        at = {"x": pl.ds(part // 2 * 2, 2), "y": pl.ds(0, 4), "z": part % 2 * 2 + j}
                        first, second, third = order_of(p, c)
                        found.append(feats[p][c, at[third], at[second], at[first], step])
                    blocks = []
                    for x_lo in range(2):
                        for c in range(2):
                            order = order_of(p, c)
                            x_outer = order.index("x") > order.index("y")
                            for y in range(4):
                                blocks.append(found[c][x_lo, y] if x_outer else found[c][y, x_lo])
                    columns.append(jnp.concatenate(blocks, axis=0))
                left = jnp.concatenate(columns, axis=1)
                weight = weights[spot]
                none = jnp.zeros((64, LANES), jnp.bfloat16)
                if k < 4:
                    weight = jnp.concatenate([weight[:64], none, weight[64:], none], axis=0)
                else:
                    weight = jnp.concatenate([none, weight[:64], none, weight[64:]], axis=0)
                term = jnp.dot(left, weight, preferred_element_type=jnp.float32)
                link = table[2, spot]
                earlier = sums[jnp.maximum(link, 0)]
                sums[spot] = term + jnp.where(link >= 0, earlier, 0.0)
            return carry

        lax.fori_loop(0, COUNTS[p], multiply, 0)

    def scatter_start(p):
        nxt, prv = rings[p][0][0], rings[p][0][2]
        one_r, one_l, two_r, two_l = lands[p][0]

        def half_of(buf, half):
            return buf.at[pl.ds(2 * half, 2)]

        def copy(number, at, half, dst, target):
            return remote(
                half_of(sends[p].at[at], half), dst,
                rs_send.at[p, 0, number], rs_recv.at[p, 0, number], target,
            )

        right, far, left = (moved(p, 0, by) for by in (1, 2, 3))
        return [
            go(copy(0, far, 0, one_r, nxt)),
            go(copy(1, far, 1, one_l, prv)),
            go(copy(2, right, 1, half_of(two_r, 1), nxt)),
            go(copy(3, left, 0, half_of(two_l, 0), prv)),
            copy(4, right, 0, half_of(two_r, 0), nxt),
            copy(5, left, 1, half_of(two_l, 1), prv),
        ]

    def scatter_direct(p, phase):
        base = tuple(spots[p][:phase])
        return [
            go(
                remote(
                    sends[p].at[base + (moved(p, phase, by + 1),)], lands[p][phase][0].at[by],
                    rs_send.at[p, phase, by], rs_recv.at[p, phase, by], rings[p][phase][by],
                )
            )
            for by in range(3)
        ]

    def add_in(p, at, half, pieces):
        offset = 2 if half == 1 else 0

        def step(k, carry):
            totals = []
            for m in range(4):
                total = sends[p][at, offset + k, m].astype(jnp.float32)
                for piece in pieces:
                    total = total + piece[k, m].astype(jnp.float32)
                totals.append(total.astype(jnp.bfloat16))
            for m in range(4):
                sends[p][at, offset + k, m] = totals[m]
            return carry

        lax.fori_loop(0, 4 if half is None else 2, step, 0)

    copies = []
    for p in range(3):

        for c in range(2):

            def lay_out(step, carry, p=p, c=c):
                for x_lo in range(2):
                    pair = []
                    for k in range(2):
                        link = table[3, x_lo * 32 + (STARTS[p] + step) * 2 + k]
                        pair.append(jnp.where(link >= 0, sums[jnp.maximum(link, 0)], 0.0))
                    for t in range(32):
                        at = {"x": t // 4 % 2 * 2 + x_lo, "y": t // 8, "z": t % 4}
                        first, second, third = order_of(p, c)
                        unit = jnp.concatenate([half[8 * t : 8 * t + 8] for half in pair], axis=0)
                        sends[p][at[first], at[second], at[third], step] = unit.astype(jnp.bfloat16)
                return carry

            @pl.when(core == c)
            def _(p=p, lay_out=lay_out):
                lax.fori_loop(0, COUNTS[p], lay_out, 0)

        copies.append(scatter_start(p))

    for p in range(3):
        copies[p][0].wait_recv()
        add_in(p, moved(p, 0, 1), 0, [lands[p][0][0]])
        go(copies[p][4])
        copies[p][1].wait_recv()
        add_in(p, moved(p, 0, 3), 1, [lands[p][0][1]])
        go(copies[p][5])
    direct = []
    for p in range(3):
        for number in (2, 3, 4, 5):
            copies[p][number].wait_recv()
        add_in(p, spots[p][0], None, lands[p][0][2:])
        direct.append(scatter_direct(p, 1))
    last = []
    for p in range(3):
        for copy in direct[p]:
            copy.wait_recv()
        base = tuple(spots[p][:2])
        totals = []
        for k in range(4):
            total = sends[p][base + (k,)].astype(jnp.float32)
            for by in range(3):
                total = total + lands[p][1][0][by, k].astype(jnp.float32)
            totals.append(total.astype(jnp.bfloat16))
        for k in range(4):
            sends[p][base + (k,)] = totals[k]
        last.append(scatter_direct(p, 2))
    for p in range(3):
        for copy in last[p]:
            copy.wait_recv()
        base = tuple(spots[p])
        for unit in range(COUNTS[p]):
            total = sends[p][base + (unit,)].astype(jnp.float32)
            for by in range(3):
                total = total + lands[p][2][0][by, unit].astype(jnp.float32)
            column = (STARTS[p] + unit) * 2 * LANES
            out[:, column : column + LANES] = total[:8].astype(jnp.bfloat16)
            out[:, column + LANES : column + 2 * LANES] = total[8:].astype(jnp.bfloat16)

    for copy in pending:
        copy.wait_send()


def scratch_shapes():
    bf16 = jnp.bfloat16
    tail = (16, LANES)
    shapes = [pltpu.VMEM((2, 4, 4, 4, n) + tail, bf16) for n in COUNTS]
    shapes += [pltpu.VMEM((4, 4, 4, n) + tail, bf16) for n in COUNTS]
    for n in COUNTS:
        shapes += [pltpu.VMEM((2, 4, n) + tail, bf16)] * 2 + [pltpu.VMEM((4, 4, n) + tail, bf16)] * 2
        shapes += [pltpu.VMEM((3, 4, n) + tail, bf16), pltpu.VMEM((3, n) + tail, bf16)]
    shapes += [
        pltpu.VMEM((2, TILES, LANES, LANES), bf16),
        pltpu.VMEM((2, TILES, LANES), jnp.float32),
        pltpu.VMEM((TILES, LANES, LANES), bf16),
        pltpu.VMEM((TILES, ROWS, LANES), jnp.float32),
        pltpu.VMEM((2, STAGE, 2048, LANES), bf16),
        pltpu.VMEM((2, STAGE, 2048, LANES), bf16),
        pltpu.VMEM((HEADS, 16, LANES), jnp.float32),
        pltpu.VMEM((TILES, LANES), bf16),
        pltpu.VMEM((16, HEADS, LANES), jnp.float32),
        pltpu.VMEM((8, TILES), jnp.int32),
        pltpu.SMEM((8, TILES), jnp.int32),
        pltpu.SemaphoreType.DMA((1,)),
        pltpu.SemaphoreType.DMA((2, 2)),
        pltpu.SemaphoreType.DMA((2,)),
        pltpu.SemaphoreType.DMA((2,)),
        pltpu.SemaphoreType.DMA((1,)),
        pltpu.SemaphoreType.DMA((3, 3, 6)),
        pltpu.SemaphoreType.DMA((3, 3, 6)),
        pltpu.SemaphoreType.DMA((3, 7)),
        pltpu.SemaphoreType.DMA((3, 7)),
        pltpu.SemaphoreType.DMA((3, 3, 6)),
        pltpu.SemaphoreType.DMA((3, 3, 6)),
    ]
    return shapes


def body(queries, cache_keys, cache_values, lengths, old_tiles, old_scales, slot_tiles):
    vmem = pl.BlockSpec(memory_space=pltpu.VMEM)
    return pl.pallas_call(
        kernel,
        out_shape=jax.ShapeDtypeStruct((8, 4096), jnp.bfloat16),
        in_specs=[
            vmem,
            pl.BlockSpec(memory_space=pltpu.SMEM),
            vmem,
            pl.BlockSpec(memory_space=pl.ANY),
            pl.BlockSpec(memory_space=pl.ANY),
            pl.BlockSpec(memory_space=pl.ANY),
            vmem,
        ],
        out_specs=vmem,
        scratch_shapes=scratch_shapes(),
        compiler_params=pltpu.CompilerParams(
            collective_id=0, has_side_effects=True, vmem_limit_bytes=58 * 2**20
        ),
    )(
        slot_tiles, lengths, queries[0], cache_keys[0], cache_values[0],
        old_tiles[0], old_scales[0],
    )


def solution(mesh):
    return jax.shard_map(
        body,
        mesh=mesh,
        in_specs=(
            P(("grp", "tp"), None, None),
            P(("grp", "tp"), None, None, None),
            P(("grp", "tp"), None, None, None),
            P(),
            P(("grp", "tp"), None, None, None),
            P(("grp", "tp"), None, None),
            P(),
        ),
        out_specs=P("tp", "grp"),
        check_vma=False,
    )
```

```python
import jax
import jax.numpy as jnp
from jax import lax
from jax.experimental import pallas as pl
from jax.experimental.pallas import tpu as pltpu
from jax.sharding import PartitionSpec as P

KV_HEADS = 8
HEAD_DIM = 128
HEADS = 16
LANES = 128
ORDERS = ("xyz", "yzx", "zxy")
COUNTS = (6, 5, 5)
STARTS = (0, 6, 11)
ROWS = 256
STAGE = 4
TILES = 128
MESH = pl.DeviceIdType.MESH


def tile_table(own, other, core):
    shape = (TILES, TILES)
    spot = lax.broadcasted_iota(jnp.int32, shape, 0)
    lane = lax.broadcasted_iota(jnp.int32, shape, 1)

    def as_row(column):
        return jnp.sum(jnp.where(spot == lane, column, 0), axis=0, keepdims=True)

    x_lo = (spot >> 1) & 1
    held = jnp.where(
        (spot & 1) == 0, jnp.broadcast_to(own, shape), jnp.broadcast_to(other, shape)
    )
    match = (held >> 7) == (x_lo * 2 + core) * 32 + (spot >> 2)
    packed = jnp.max(jnp.where(match, lane * 128 + (held & 127), 0), axis=1, keepdims=True)
    packed = jnp.broadcast_to(packed, shape)
    key = x_lo * 32 + (packed & 31)
    key_row = jnp.broadcast_to(as_row(key), shape)
    before = (key_row == key) & (lane < spot)
    previous = jnp.max(jnp.where(before, lane, -1), axis=1, keepdims=True)
    last = jnp.max(jnp.where(key_row == spot, lane, -1), axis=1, keepdims=True)
    return [
        as_row(packed >> 7),
        as_row((packed >> 5) & 3),
        as_row(jnp.broadcast_to(previous, shape)),
        as_row(jnp.broadcast_to(last, shape)),
    ]


def order_of(p, core):
    return ORDERS[(p + core) % 3]


def kernel(*refs):
    slot_tiles, lengths, queries, keys, values, tiles_own, scales_own, out = refs[:8]
    scratch = list(refs[8:])
    feats = [scratch.pop(0) for _ in range(3)]
    sends = [scratch.pop(0) for _ in range(3)]
    lands = [[[scratch.pop(0) for _ in range(many)] for many in (4, 1, 1)] for _ in range(3)]
    tiles, scales, weights, sums = [scratch.pop(0) for _ in range(4)]
    key_buf, value_buf, att, scales_other, by_row = [scratch.pop(0) for _ in range(5)]
    table_vmem, table, table_sem = [scratch.pop(0) for _ in range(3)]
    kv_sem, swap_send, swap_recv = [scratch.pop(0) for _ in range(3)]
    load_sem, ag_send, ag_recv, sib_send, sib_recv, rs_send, rs_recv = scratch

    grp, tp = lax.axis_index("grp"), lax.axis_index("tp")
    core = lax.rem(grp, 2)
    me = {"x": lax.rem(lax.div(tp, 4), 2) * 2 + lax.div(grp, 2), "y": lax.div(tp, 8), "z": lax.rem(tp, 4)}

    def shifted(axis, by):
        return lax.rem(me[axis] + by, 4)

    def device(axis, by):
        at = dict(me)
        at[axis] = shifted(axis, by)
        return (
            lax.rem(at["x"], 2) * 2 + core,
            at["y"] * 8 + lax.div(at["x"], 2) * 4 + at["z"],
        )

    ring = {axis: [device(axis, by) for by in (1, 2, 3)] for axis in "xyz"}

    def either(a, b):
        return jnp.where(core == 0, a, b)

    spots, rings = [], []
    for p in range(3):
        mine = list(zip(order_of(p, 0), order_of(p, 1)))
        spots.append([either(me[a], me[b]) for a, b in mine])
        rings.append(
            [[tuple(map(either, ring[a][by], ring[b][by])) for by in range(3)] for a, b in mine]
        )

    def moved(p, phase, by):
        return lax.rem(spots[p][phase] + by, 4)

    sibling = (grp + 1 - 2 * core, tp)

    def kv_load(stage, slot):
        rows = pl.ds(stage * STAGE, STAGE)
        return [
            pltpu.make_async_copy(keys.at[rows], key_buf.at[slot], kv_sem.at[slot, 0]),
            pltpu.make_async_copy(values.at[rows], value_buf.at[slot], kv_sem.at[slot, 1]),
        ]

    for stage in range(2):
        for load in kv_load(stage, stage):
            load.start()
    loads = [pltpu.make_async_copy(tiles_own, tiles.at[0], load_sem.at[0])]

    barrier = pltpu.get_barrier_semaphore()
    for other in [*ring["x"], *ring["y"], *ring["z"], sibling]:
        pl.semaphore_signal(barrier, inc=1, device_id=other, device_id_type=MESH)

    def remote(src, dst, send, recv, target):
        return pltpu.make_async_remote_copy(
            src_ref=src, dst_ref=dst, send_sem=send, recv_sem=recv,
            device_id=target, device_id_type=MESH,
        )

    pending = []

    def go(copy):
        copy.start()
        pending.append(copy)
        return copy

    own = slot_tiles[pl.ds(grp * 32 + tp, 1), :]
    other = slot_tiles[pl.ds((grp + 1 - 2 * core) * 32 + tp, 1), :]
    for number, row in enumerate(tile_table(own, other, core)):
        table_vmem[number : number + 1, :] = row
    table_load = pltpu.make_async_copy(table_vmem, table, table_sem.at[0])
    table_load.start()

    for h in range(HEADS):
        head = queries[:, h * HEAD_DIM : (h + 1) * HEAD_DIM].astype(jnp.float32)
        by_row[:, h : h + 1, :] = head[:, None, :]
    first_row = lax.div(grp * 32 + tp, KV_HEADS) * 16

    def attend(stage, carry):
        slot = lax.rem(stage, 2)
        for load in kv_load(stage, slot):
            load.wait()
        live, masses = [], []
        for k in range(STAGE):
            row = stage * STAGE + k
            scores = lax.dot_general(
                by_row[row].astype(jnp.bfloat16), key_buf[slot, k], (((1,), (1,)), ((), ())),
                preferred_element_type=jnp.float32,
            ) * HEAD_DIM ** (-0.5)
            live.append(scores)
        for k in range(STAGE):
            row = stage * STAGE + k
            inside = lax.broadcasted_iota(jnp.int32, live[k].shape, 1) < lengths[first_row + row]
            scores = jnp.where(inside, live[k], -1e30)
            row_max = jnp.max(scores, axis=1, keepdims=True)
            mass = jnp.where(inside, jnp.exp(scores - row_max), 0.0)
            share = 1.0 / jnp.sum(mass, axis=1, keepdims=True)
            masses.append((mass * share).astype(jnp.bfloat16))
        for k in range(STAGE):
            row = stage * STAGE + k
            mixed = jnp.dot(masses[k], value_buf[slot, k], preferred_element_type=jnp.float32)
            att[:, pl.ds(row, 1), :] = mixed[:, None, :]

        @pl.when(stage < 16 // STAGE - 2)
        def _():
            for load in kv_load(stage + 2, slot):
                load.start()

        return carry

    lax.fori_loop(0, 16 // STAGE, attend, 0)
    for load in loads:
        load.start()
    pl.semaphore_wait(barrier, 10)
    def gather_view(p, at, half):
        return feats[p].at[core, at, pl.ds(2 * half, 2)]

    def gather_direct(p, phase):
        first, second, third = spots[p]
        view = feats[p].at[core, third, second, first] if phase == 0 else feats[p].at[core, third, second]
        return [
            go(remote(view, view, ag_send.at[p, phase, by], ag_recv.at[p, phase, by], rings[p][phase][by]))
            for by in range(3)
        ]

    def gather_copy(p, number, at, half, target):
        view = gather_view(p, at, half)
        return go(remote(view, view, ag_send.at[p, 2, number], ag_recv.at[p, 2, number], target))

    def pass_on(p, number, view):
        go(remote(view, view, sib_send.at[p, number], sib_recv.at[p, number], sibling))

    def gather_start(p):
        here = spots[p][2]
        nxt, prv = rings[p][2][0], rings[p][2][2]
        return [
            gather_copy(p, 0, here, 0, nxt),
            gather_copy(p, 1, here, 1, prv),
            gather_copy(p, 2, here, 1, nxt),
            gather_copy(p, 3, here, 0, prv),
        ]

    def gather_forward(p, found):
        nxt, prv = rings[p][2][0], rings[p][2][2]
        found[0].wait_recv()
        found.append(gather_copy(p, 4, moved(p, 2, 3), 0, nxt))
        found[1].wait_recv()
        found.append(gather_copy(p, 5, moved(p, 2, 1), 1, prv))

    begun = []
    for p in range(3):
        first, second, third = spots[p]
        feats[p][core, third, second, first] = att[STARTS[p] : STARTS[p] + COUNTS[p]].astype(jnp.bfloat16)
        begun.append(gather_direct(p, 0))
    swaps = [
        go(remote(tiles_own, tiles.at[1], swap_send.at[0], swap_recv.at[0], sibling)),
        go(remote(scales_own, scales_other, swap_send.at[1], swap_recv.at[1], sibling)),
    ]
    across = []
    for p in range(3):
        for copy in begun[p]:
            copy.wait_recv()
        across.append(gather_direct(p, 1))
    founds = []
    for p in range(3):
        for copy in across[p]:
            copy.wait_recv()
        founds.append(gather_start(p))
        pass_on(p, 0, feats[p].at[core, spots[p][2]])
    for p in range(3):
        gather_forward(p, founds[p])
        pass_on(p, 1, gather_view(p, moved(p, 2, 3), 0))
        pass_on(p, 2, gather_view(p, moved(p, 2, 1), 1))
    for load in loads:
        load.wait()
    table_load.wait()
    for swap in swaps:
        swap.wait_recv()
    scales[0] = scales_own[...].astype(jnp.float32)
    scales[1] = scales_other[...].astype(jnp.float32)
    diagonal = lax.broadcasted_iota(jnp.int32, (LANES, LANES), 0) == lax.broadcasted_iota(
        jnp.int32, (LANES, LANES), 1
    )

    def dequantize(step, carry):
        for k in range(8):
            spot = step * 8 + k
            where = table[0, spot]
            row = scales[k % 2, pl.ds(where, 1), :]
            spread = jnp.where(diagonal, jnp.broadcast_to(row, (LANES, LANES)), 0.0)
            weights[spot] = jnp.dot(
                spread.astype(jnp.bfloat16), tiles[k % 2, where],
                preferred_element_type=jnp.float32,
            ).astype(jnp.bfloat16)
        return carry

    lax.fori_loop(0, TILES // 8, dequantize, 0)
    for numbers, p in [((2, 3), p) for p in range(3)] + [((4, 5), p) for p in range(3)]:
        for number in numbers:
            founds[p][number].wait_recv()
            by, half = ((3, 1), (1, 0), (2, 0), (2, 1))[number - 2]
            pass_on(p, number + 1, gather_view(p, moved(p, 2, by), half))

    for p in range(3):
        for number in range(7):
            size = feats[p].at[core, 0] if number == 0 else feats[p].at[core, 0, pl.ds(0, 2)]
            remote(size, size, sib_send.at[p, number], sib_recv.at[p, number], sibling).wait_recv()

        def multiply(step, carry, p=p):
            terms = []
            for k in range(8):
                spot = (STARTS[p] + step) * 8 + k
                part = table[1, spot]
                columns = []
                for j in range(2):
                    found = []
                    for c in range(2):
                        at = {"x": pl.ds(part // 2 * 2, 2), "y": pl.ds(0, 4), "z": part % 2 * 2 + j}
                        first, second, third = order_of(p, c)
                        found.append(feats[p][c, at[third], at[second], at[first], step])
                    blocks = []
                    for x_lo in range(2):
                        for c in range(2):
                            order = order_of(p, c)
                            x_outer = order.index("x") > order.index("y")
                            for y in range(4):
                                blocks.append(found[c][x_lo, y] if x_outer else found[c][y, x_lo])
                    columns.append(jnp.concatenate(blocks, axis=0))
                left = jnp.concatenate(columns, axis=1)
                weight = weights[spot]
                none = jnp.zeros((64, LANES), jnp.bfloat16)
                if k < 4:
                    weight = jnp.concatenate([weight[:64], none, weight[64:], none], axis=0)
                else:
                    weight = jnp.concatenate([none, weight[:64], none, weight[64:]], axis=0)
                terms.append((spot, jnp.dot(left, weight, preferred_element_type=jnp.float32)))
                if k % 8 == 7:
                    for spot, term in terms:
                        link = table[2, spot]
                        earlier = sums[jnp.maximum(link, 0)]
                        sums[spot] = term + jnp.where(link >= 0, earlier, 0.0)
                    terms = []
            return carry

        lax.fori_loop(0, COUNTS[p], multiply, 0)

    def scatter_start(p):
        nxt, prv = rings[p][0][0], rings[p][0][2]
        one_r, one_l, two_r, two_l = lands[p][0]

        def half_of(buf, half):
            return buf.at[pl.ds(2 * half, 2)]

        def copy(number, at, half, dst, target):
            return remote(
                half_of(sends[p].at[at], half), dst,
                rs_send.at[p, 0, number], rs_recv.at[p, 0, number], target,
            )

        right, far, left = (moved(p, 0, by) for by in (1, 2, 3))
        return [
            go(copy(0, far, 0, one_r, nxt)),
            go(copy(1, far, 1, one_l, prv)),
            go(copy(2, right, 1, half_of(two_r, 1), nxt)),
            go(copy(3, left, 0, half_of(two_l, 0), prv)),
            copy(4, right, 0, half_of(two_r, 0), nxt),
            copy(5, left, 1, half_of(two_l, 1), prv),
        ]

    def scatter_direct(p, phase):
        base = tuple(spots[p][:phase])
        return [
            go(
                remote(
                    sends[p].at[base + (moved(p, phase, by + 1),)], lands[p][phase][0].at[by],
                    rs_send.at[p, phase, by], rs_recv.at[p, phase, by], rings[p][phase][by],
                )
            )
            for by in range(3)
        ]

    def add_in(p, at, half, pieces):
        offset = 2 if half == 1 else 0

        def step(k, carry):
            totals = []
            for m in range(4):
                total = sends[p][at, offset + k, m].astype(jnp.float32)
                for piece in pieces:
                    total = total + piece[k, m].astype(jnp.float32)
                totals.append(total.astype(jnp.bfloat16))
            for m in range(4):
                sends[p][at, offset + k, m] = totals[m]
            return carry

        lax.fori_loop(0, 4 if half is None else 2, step, 0)

    copies = []
    for p in range(3):

        for c in range(2):

            def lay_out(step, carry, p=p, c=c):
                for x_lo in range(2):
                    pair = []
                    for k in range(2):
                        link = table[3, x_lo * 32 + (STARTS[p] + step) * 2 + k]
                        pair.append(jnp.where(link >= 0, sums[jnp.maximum(link, 0)], 0.0))
                    for t in range(32):
                        at = {"x": t // 4 % 2 * 2 + x_lo, "y": t // 8, "z": t % 4}
                        first, second, third = order_of(p, c)
                        unit = jnp.concatenate([half[8 * t : 8 * t + 8] for half in pair], axis=0)
                        sends[p][at[first], at[second], at[third], step] = unit.astype(jnp.bfloat16)
                return carry

            @pl.when(core == c)
            def _(p=p, lay_out=lay_out):
                lax.fori_loop(0, COUNTS[p], lay_out, 0)

        copies.append(scatter_start(p))

    for p in range(3):
        copies[p][0].wait_recv()
        add_in(p, moved(p, 0, 1), 0, [lands[p][0][0]])
        go(copies[p][4])
        copies[p][1].wait_recv()
        add_in(p, moved(p, 0, 3), 1, [lands[p][0][1]])
        go(copies[p][5])
    direct = []
    for p in range(3):
        for number in (2, 3, 4, 5):
            copies[p][number].wait_recv()
        add_in(p, spots[p][0], None, lands[p][0][2:])
        direct.append(scatter_direct(p, 1))
    last = []
    for p in range(3):
        for copy in direct[p]:
            copy.wait_recv()
        base = tuple(spots[p][:2])
        totals = []
        for k in range(4):
            total = sends[p][base + (k,)].astype(jnp.float32)
            for by in range(3):
                total = total + lands[p][1][0][by, k].astype(jnp.float32)
            totals.append(total.astype(jnp.bfloat16))
        for k in range(4):
            sends[p][base + (k,)] = totals[k]
        last.append(scatter_direct(p, 2))
    for p in range(3):
        for copy in last[p]:
            copy.wait_recv()
        base = tuple(spots[p])
        for unit in range(COUNTS[p]):
            total = sends[p][base + (unit,)].astype(jnp.float32)
            for by in range(3):
                total = total + lands[p][2][0][by, unit].astype(jnp.float32)
            column = (STARTS[p] + unit) * 2 * LANES
            out[:, column : column + LANES] = total[:8].astype(jnp.bfloat16)
            out[:, column + LANES : column + 2 * LANES] = total[8:].astype(jnp.bfloat16)

    for copy in pending:
        copy.wait_send()


def scratch_shapes():
    bf16 = jnp.bfloat16
    tail = (16, LANES)
    shapes = [pltpu.VMEM((2, 4, 4, 4, n) + tail, bf16) for n in COUNTS]
    shapes += [pltpu.VMEM((4, 4, 4, n) + tail, bf16) for n in COUNTS]
    for n in COUNTS:
        shapes += [pltpu.VMEM((2, 4, n) + tail, bf16)] * 2 + [pltpu.VMEM((4, 4, n) + tail, bf16)] * 2
        shapes += [pltpu.VMEM((3, 4, n) + tail, bf16), pltpu.VMEM((3, n) + tail, bf16)]
    shapes += [
        pltpu.VMEM((2, TILES, LANES, LANES), bf16),
        pltpu.VMEM((2, TILES, LANES), jnp.float32),
        pltpu.VMEM((TILES, LANES, LANES), bf16),
        pltpu.VMEM((TILES, ROWS, LANES), jnp.float32),
        pltpu.VMEM((2, STAGE, 2048, LANES), bf16),
        pltpu.VMEM((2, STAGE, 2048, LANES), bf16),
        pltpu.VMEM((HEADS, 16, LANES), jnp.float32),
        pltpu.VMEM((TILES, LANES), bf16),
        pltpu.VMEM((16, HEADS, LANES), jnp.float32),
        pltpu.VMEM((8, TILES), jnp.int32),
        pltpu.SMEM((8, TILES), jnp.int32),
        pltpu.SemaphoreType.DMA((1,)),
        pltpu.SemaphoreType.DMA((2, 2)),
        pltpu.SemaphoreType.DMA((2,)),
        pltpu.SemaphoreType.DMA((2,)),
        pltpu.SemaphoreType.DMA((1,)),
        pltpu.SemaphoreType.DMA((3, 3, 6)),
        pltpu.SemaphoreType.DMA((3, 3, 6)),
        pltpu.SemaphoreType.DMA((3, 7)),
        pltpu.SemaphoreType.DMA((3, 7)),
        pltpu.SemaphoreType.DMA((3, 3, 6)),
        pltpu.SemaphoreType.DMA((3, 3, 6)),
    ]
    return shapes


def body(queries, cache_keys, cache_values, lengths, old_tiles, old_scales, slot_tiles):
    vmem = pl.BlockSpec(memory_space=pltpu.VMEM)
    return pl.pallas_call(
        kernel,
        out_shape=jax.ShapeDtypeStruct((8, 4096), jnp.bfloat16),
        in_specs=[
            vmem,
            pl.BlockSpec(memory_space=pltpu.SMEM),
            vmem,
            pl.BlockSpec(memory_space=pl.ANY),
            pl.BlockSpec(memory_space=pl.ANY),
            pl.BlockSpec(memory_space=pl.ANY),
            vmem,
        ],
        out_specs=vmem,
        scratch_shapes=scratch_shapes(),
        compiler_params=pltpu.CompilerParams(
            collective_id=0, has_side_effects=True, vmem_limit_bytes=58 * 2**20
        ),
    )(
        slot_tiles, lengths, queries[0], cache_keys[0], cache_values[0],
        old_tiles[0], old_scales[0],
    )


def solution(mesh):
    return jax.shard_map(
        body,
        mesh=mesh,
        in_specs=(
            P(("grp", "tp"), None, None),
            P(("grp", "tp"), None, None, None),
            P(("grp", "tp"), None, None, None),
            P(),
            P(("grp", "tp"), None, None, None),
            P(("grp", "tp"), None, None),
            P(),
        ),
        out_specs=P("tp", "grp"),
        check_vma=False,
    )
```

```python
import jax
import jax.numpy as jnp
from jax import lax
from jax.experimental import pallas as pl
from jax.experimental.pallas import tpu as pltpu
from jax.sharding import PartitionSpec as P

KV_HEADS = 8
HEAD_DIM = 128
HEADS = 16
LANES = 128
ORDERS = ("xyz", "yzx", "zxy")
COUNTS = (6, 5, 5)
STARTS = (0, 6, 11)
ROWS = 256
STAGE = 4
TILES = 128
MESH = pl.DeviceIdType.MESH


def tile_table(own, other, core):
    shape = (TILES, TILES)
    spot = lax.broadcasted_iota(jnp.int32, shape, 0)
    lane = lax.broadcasted_iota(jnp.int32, shape, 1)

    def as_row(column):
        return jnp.sum(jnp.where(spot == lane, column, 0), axis=0, keepdims=True)

    x_lo = (spot >> 1) & 1
    held = jnp.where(
        (spot & 1) == 0, jnp.broadcast_to(own, shape), jnp.broadcast_to(other, shape)
    )
    match = (held >> 7) == (x_lo * 2 + core) * 32 + (spot >> 2)
    packed = jnp.max(jnp.where(match, lane * 128 + (held & 127), 0), axis=1, keepdims=True)
    packed = jnp.broadcast_to(packed, shape)
    key = x_lo * 32 + (packed & 31)
    key_row = jnp.broadcast_to(as_row(key), shape)
    before = (key_row == key) & (lane < spot)
    previous = jnp.max(jnp.where(before, lane, -1), axis=1, keepdims=True)
    last = jnp.max(jnp.where(key_row == spot, lane, -1), axis=1, keepdims=True)
    return [
        as_row(packed >> 7),
        as_row((packed >> 5) & 3),
        as_row(jnp.broadcast_to(previous, shape)),
        as_row(jnp.broadcast_to(last, shape)),
    ]


def order_of(p, core):
    return ORDERS[(p + core) % 3]


def kernel(*refs):
    slot_tiles, lengths, queries, keys, values, tiles_own, scales_own, out = refs[:8]
    scratch = list(refs[8:])
    feats = [scratch.pop(0) for _ in range(3)]
    sends = [scratch.pop(0) for _ in range(3)]
    lands = [[[scratch.pop(0) for _ in range(many)] for many in (4, 1, 1)] for _ in range(3)]
    tiles, scales, weights, sums = [scratch.pop(0) for _ in range(4)]
    key_buf, value_buf, att, scales_other, by_row = [scratch.pop(0) for _ in range(5)]
    table_vmem, table, table_sem = [scratch.pop(0) for _ in range(3)]
    kv_sem, swap_send, swap_recv = [scratch.pop(0) for _ in range(3)]
    load_sem, ag_send, ag_recv, sib_send, sib_recv, rs_send, rs_recv = scratch

    grp, tp = lax.axis_index("grp"), lax.axis_index("tp")
    core = lax.rem(grp, 2)
    me = {"x": lax.rem(lax.div(tp, 4), 2) * 2 + lax.div(grp, 2), "y": lax.div(tp, 8), "z": lax.rem(tp, 4)}

    def shifted(axis, by):
        return lax.rem(me[axis] + by, 4)

    def device(axis, by):
        at = dict(me)
        at[axis] = shifted(axis, by)
        return (
            lax.rem(at["x"], 2) * 2 + core,
            at["y"] * 8 + lax.div(at["x"], 2) * 4 + at["z"],
        )

    ring = {axis: [device(axis, by) for by in (1, 2, 3)] for axis in "xyz"}

    def either(a, b):
        return jnp.where(core == 0, a, b)

    spots, rings = [], []
    for p in range(3):
        mine = list(zip(order_of(p, 0), order_of(p, 1)))
        spots.append([either(me[a], me[b]) for a, b in mine])
        rings.append(
            [[tuple(map(either, ring[a][by], ring[b][by])) for by in range(3)] for a, b in mine]
        )

    def moved(p, phase, by):
        return lax.rem(spots[p][phase] + by, 4)

    sibling = (grp + 1 - 2 * core, tp)

    def kv_load(stage, slot):
        rows = pl.ds(stage * STAGE, STAGE)
        return [
            pltpu.make_async_copy(keys.at[rows], key_buf.at[slot], kv_sem.at[slot, 0]),
            pltpu.make_async_copy(values.at[rows], value_buf.at[slot], kv_sem.at[slot, 1]),
        ]

    for stage in range(2):
        for load in kv_load(stage, stage):
            load.start()
    loads = [pltpu.make_async_copy(tiles_own, tiles.at[0], load_sem.at[0])]

    barrier = pltpu.get_barrier_semaphore()
    for other in [*ring["x"], *ring["y"], *ring["z"], sibling]:
        pl.semaphore_signal(barrier, inc=1, device_id=other, device_id_type=MESH)

    def remote(src, dst, send, recv, target):
        return pltpu.make_async_remote_copy(
            src_ref=src, dst_ref=dst, send_sem=send, recv_sem=recv,
            device_id=target, device_id_type=MESH,
        )

    pending = []

    def go(copy):
        copy.start()
        pending.append(copy)
        return copy

    own = slot_tiles[pl.ds(grp * 32 + tp, 1), :]
    other = slot_tiles[pl.ds((grp + 1 - 2 * core) * 32 + tp, 1), :]
    for number, row in enumerate(tile_table(own, other, core)):
        table_vmem[number : number + 1, :] = row
    table_load = pltpu.make_async_copy(table_vmem, table, table_sem.at[0])
    table_load.start()

    for h in range(HEADS):
        head = queries[:, h * HEAD_DIM : (h + 1) * HEAD_DIM].astype(jnp.float32)
        by_row[:, h : h + 1, :] = head[:, None, :]
    first_row = lax.div(grp * 32 + tp, KV_HEADS) * 16

    def attend(stage, carry):
        slot = lax.rem(stage, 2)
        for load in kv_load(stage, slot):
            load.wait()
        live, masses = [], []
        for k in range(STAGE):
            row = stage * STAGE + k
            scores = lax.dot_general(
                by_row[row].astype(jnp.bfloat16), key_buf[slot, k], (((1,), (1,)), ((), ())),
                preferred_element_type=jnp.float32,
            ) * HEAD_DIM ** (-0.5)
            live.append(scores)
        for k in range(STAGE):
            row = stage * STAGE + k
            inside = lax.broadcasted_iota(jnp.int32, live[k].shape, 1) < lengths[first_row + row]
            scores = jnp.where(inside, live[k], -1e30)
            row_max = jnp.max(scores, axis=1, keepdims=True)
            mass = jnp.where(inside, jnp.exp(scores - row_max), 0.0)
            share = 1.0 / jnp.sum(mass, axis=1, keepdims=True)
            masses.append((mass * share).astype(jnp.bfloat16))
        for k in range(STAGE):
            row = stage * STAGE + k
            mixed = jnp.dot(masses[k], value_buf[slot, k], preferred_element_type=jnp.float32)
            att[:, pl.ds(row, 1), :] = mixed[:, None, :]

        @pl.when(stage < 16 // STAGE - 2)
        def _():
            for load in kv_load(stage + 2, slot):
                load.start()

        return carry

    lax.fori_loop(0, 16 // STAGE, attend, 0)
    for load in loads:
        load.start()
    pl.semaphore_wait(barrier, 10)
    def gather_view(p, at, half):
        return feats[p].at[core, at, pl.ds(2 * half, 2)]

    def gather_direct(p, phase):
        first, second, third = spots[p]
        view = feats[p].at[core, third, second, first] if phase == 0 else feats[p].at[core, third, second]
        return [
            go(remote(view, view, ag_send.at[p, phase, by], ag_recv.at[p, phase, by], rings[p][phase][by]))
            for by in range(3)
        ]

    def gather_copy(p, number, at, half, target):
        view = gather_view(p, at, half)
        return go(remote(view, view, ag_send.at[p, 2, number], ag_recv.at[p, 2, number], target))

    def pass_on(p, number, view):
        go(remote(view, view, sib_send.at[p, number], sib_recv.at[p, number], sibling))

    def gather_start(p):
        here = spots[p][2]
        nxt, prv = rings[p][2][0], rings[p][2][2]
        return [
            gather_copy(p, 0, here, 0, nxt),
            gather_copy(p, 1, here, 1, prv),
            gather_copy(p, 2, here, 1, nxt),
            gather_copy(p, 3, here, 0, prv),
        ]

    def gather_forward(p, found):
        nxt, prv = rings[p][2][0], rings[p][2][2]
        found[0].wait_recv()
        found.append(gather_copy(p, 4, moved(p, 2, 3), 0, nxt))
        found[1].wait_recv()
        found.append(gather_copy(p, 5, moved(p, 2, 1), 1, prv))

    begun = []
    for p in range(3):
        first, second, third = spots[p]
        feats[p][core, third, second, first] = att[STARTS[p] : STARTS[p] + COUNTS[p]].astype(jnp.bfloat16)
        begun.append(gather_direct(p, 0))
    swaps = [
        go(remote(tiles_own, tiles.at[1], swap_send.at[0], swap_recv.at[0], sibling)),
        go(remote(scales_own, scales_other, swap_send.at[1], swap_recv.at[1], sibling)),
    ]
    across = []
    for p in range(3):
        for copy in begun[p]:
            copy.wait_recv()
        across.append(gather_direct(p, 1))
    founds = []
    for p in range(3):
        for copy in across[p]:
            copy.wait_recv()
        founds.append(gather_start(p))
        pass_on(p, 0, feats[p].at[core, spots[p][2]])
    for p in range(3):
        gather_forward(p, founds[p])
        pass_on(p, 1, gather_view(p, moved(p, 2, 3), 0))
        pass_on(p, 2, gather_view(p, moved(p, 2, 1), 1))
    for load in loads:
        load.wait()
    table_load.wait()
    for swap in swaps:
        swap.wait_recv()
    scales[0] = scales_own[...].astype(jnp.float32)
    scales[1] = scales_other[...].astype(jnp.float32)
    diagonal = lax.broadcasted_iota(jnp.int32, (LANES, LANES), 0) == lax.broadcasted_iota(
        jnp.int32, (LANES, LANES), 1
    )

    def dequantize(step, carry):
        for k in range(8):
            spot = step * 8 + k
            where = table[0, spot]
            row = scales[k % 2, pl.ds(where, 1), :]
            spread = jnp.where(diagonal, jnp.broadcast_to(row, (LANES, LANES)), 0.0)
            weights[spot] = jnp.dot(
                spread.astype(jnp.bfloat16), tiles[k % 2, where],
                preferred_element_type=jnp.float32,
            ).astype(jnp.bfloat16)
        return carry

    lax.fori_loop(0, TILES // 8, dequantize, 0)
    for p in range(3):
        for number in (2, 3, 4, 5):
            founds[p][number].wait_recv()
            by, half = ((3, 1), (1, 0), (2, 0), (2, 1))[number - 2]
            pass_on(p, number + 1, gather_view(p, moved(p, 2, by), half))

    for p in range(3):
        for number in range(7):
            size = feats[p].at[core, 0] if number == 0 else feats[p].at[core, 0, pl.ds(0, 2)]
            remote(size, size, sib_send.at[p, number], sib_recv.at[p, number], sibling).wait_recv()

        def multiply(step, carry, p=p):
            terms = []
            for k in range(8):
                spot = (STARTS[p] + step) * 8 + k
                part = table[1, spot]
                columns = []
                for j in range(2):
                    found = []
                    for c in range(2):
                        at = {"x": pl.ds(part // 2 * 2, 2), "y": pl.ds(0, 4), "z": part % 2 * 2 + j}
                        first, second, third = order_of(p, c)
                        found.append(feats[p][c, at[third], at[second], at[first], step])
                    blocks = []
                    for x_lo in range(2):
                        for c in range(2):
                            order = order_of(p, c)
                            x_outer = order.index("x") > order.index("y")
                            for y in range(4):
                                blocks.append(found[c][x_lo, y] if x_outer else found[c][y, x_lo])
                    columns.append(jnp.concatenate(blocks, axis=0))
                left = jnp.concatenate(columns, axis=1)
                weight = weights[spot]
                none = jnp.zeros((64, LANES), jnp.bfloat16)
                if k < 4:
                    weight = jnp.concatenate([weight[:64], none, weight[64:], none], axis=0)
                else:
                    weight = jnp.concatenate([none, weight[:64], none, weight[64:]], axis=0)
                terms.append((spot, jnp.dot(left, weight, preferred_element_type=jnp.float32)))
                if k % 8 == 7:
                    for spot, term in terms:
                        link = table[2, spot]
                        earlier = sums[jnp.maximum(link, 0)]
                        sums[spot] = term + jnp.where(link >= 0, earlier, 0.0)
                    terms = []
            return carry

        lax.fori_loop(0, COUNTS[p], multiply, 0)

    def scatter_start(p):
        nxt, prv = rings[p][0][0], rings[p][0][2]
        one_r, one_l, two_r, two_l = lands[p][0]

        def half_of(buf, half):
            return buf.at[pl.ds(2 * half, 2)]

        def copy(number, at, half, dst, target):
            return remote(
                half_of(sends[p].at[at], half), dst,
                rs_send.at[p, 0, number], rs_recv.at[p, 0, number], target,
            )

        right, far, left = (moved(p, 0, by) for by in (1, 2, 3))
        return [
            go(copy(0, far, 0, one_r, nxt)),
            go(copy(1, far, 1, one_l, prv)),
            go(copy(2, right, 1, half_of(two_r, 1), nxt)),
            go(copy(3, left, 0, half_of(two_l, 0), prv)),
            copy(4, right, 0, half_of(two_r, 0), nxt),
            copy(5, left, 1, half_of(two_l, 1), prv),
        ]

    def scatter_direct(p, phase):
        base = tuple(spots[p][:phase])
        return [
            go(
                remote(
                    sends[p].at[base + (moved(p, phase, by + 1),)], lands[p][phase][0].at[by],
                    rs_send.at[p, phase, by], rs_recv.at[p, phase, by], rings[p][phase][by],
                )
            )
            for by in range(3)
        ]

    def add_in(p, at, half, pieces):
        offset = 2 if half == 1 else 0

        def step(k, carry):
            totals = []
            for m in range(4):
                total = sends[p][at, offset + k, m].astype(jnp.float32)
                for piece in pieces:
                    total = total + piece[k, m].astype(jnp.float32)
                totals.append(total.astype(jnp.bfloat16))
            for m in range(4):
                sends[p][at, offset + k, m] = totals[m]
            return carry

        lax.fori_loop(0, 4 if half is None else 2, step, 0)

    copies = []
    for p in range(3):

        for c in range(2):

            def lay_out(step, carry, p=p, c=c):
                for x_lo in range(2):
                    pair = []
                    for k in range(2):
                        link = table[3, x_lo * 32 + (STARTS[p] + step) * 2 + k]
                        pair.append(jnp.where(link >= 0, sums[jnp.maximum(link, 0)], 0.0))
                    for t in range(32):
                        at = {"x": t // 4 % 2 * 2 + x_lo, "y": t // 8, "z": t % 4}
                        first, second, third = order_of(p, c)
                        unit = jnp.concatenate([half[8 * t : 8 * t + 8] for half in pair], axis=0)
                        sends[p][at[first], at[second], at[third], step] = unit.astype(jnp.bfloat16)
                return carry

            @pl.when(core == c)
            def _(p=p, lay_out=lay_out):
                lax.fori_loop(0, COUNTS[p], lay_out, 0)

        copies.append(scatter_start(p))

    for p in range(3):
        copies[p][0].wait_recv()
        add_in(p, moved(p, 0, 1), 0, [lands[p][0][0]])
        go(copies[p][4])
        copies[p][1].wait_recv()
        add_in(p, moved(p, 0, 3), 1, [lands[p][0][1]])
        go(copies[p][5])
    direct = []
    for p in range(3):
        for number in (2, 3, 4, 5):
            copies[p][number].wait_recv()
        add_in(p, spots[p][0], None, lands[p][0][2:])
        direct.append(scatter_direct(p, 1))
    last = []
    for p in range(3):
        for copy in direct[p]:
            copy.wait_recv()
        base = tuple(spots[p][:2])
        totals = []
        for k in range(4):
            total = sends[p][base + (k,)].astype(jnp.float32)
            for by in range(3):
                total = total + lands[p][1][0][by, k].astype(jnp.float32)
            totals.append(total.astype(jnp.bfloat16))
        for k in range(4):
            sends[p][base + (k,)] = totals[k]
        last.append(scatter_direct(p, 2))
    for p in range(3):
        for copy in last[p]:
            copy.wait_recv()
        base = tuple(spots[p])
        for unit in range(COUNTS[p]):
            total = sends[p][base + (unit,)].astype(jnp.float32)
            for by in range(3):
                total = total + lands[p][2][0][by, unit].astype(jnp.float32)
            column = (STARTS[p] + unit) * 2 * LANES
            out[:, column : column + LANES] = total[:8].astype(jnp.bfloat16)
            out[:, column + LANES : column + 2 * LANES] = total[8:].astype(jnp.bfloat16)

    for copy in pending:
        copy.wait_send()


def scratch_shapes():
    bf16 = jnp.bfloat16
    tail = (16, LANES)
    shapes = [pltpu.VMEM((2, 4, 4, 4, n) + tail, bf16) for n in COUNTS]
    shapes += [pltpu.VMEM((4, 4, 4, n) + tail, bf16) for n in COUNTS]
    for n in COUNTS:
        shapes += [pltpu.VMEM((2, 4, n) + tail, bf16)] * 2 + [pltpu.VMEM((4, 4, n) + tail, bf16)] * 2
        shapes += [pltpu.VMEM((3, 4, n) + tail, bf16), pltpu.VMEM((3, n) + tail, bf16)]
    shapes += [
        pltpu.VMEM((2, TILES, LANES, LANES), bf16),
        pltpu.VMEM((2, TILES, LANES), jnp.float32),
        pltpu.VMEM((TILES, LANES, LANES), bf16),
        pltpu.VMEM((TILES, ROWS, LANES), jnp.float32),
        pltpu.VMEM((2, STAGE, 2048, LANES), bf16),
        pltpu.VMEM((2, STAGE, 2048, LANES), bf16),
        pltpu.VMEM((HEADS, 16, LANES), jnp.float32),
        pltpu.VMEM((TILES, LANES), bf16),
        pltpu.VMEM((16, HEADS, LANES), jnp.float32),
        pltpu.VMEM((8, TILES), jnp.int32),
        pltpu.SMEM((8, TILES), jnp.int32),
        pltpu.SemaphoreType.DMA((1,)),
        pltpu.SemaphoreType.DMA((2, 2)),
        pltpu.SemaphoreType.DMA((2,)),
        pltpu.SemaphoreType.DMA((2,)),
        pltpu.SemaphoreType.DMA((1,)),
        pltpu.SemaphoreType.DMA((3, 3, 6)),
        pltpu.SemaphoreType.DMA((3, 3, 6)),
        pltpu.SemaphoreType.DMA((3, 7)),
        pltpu.SemaphoreType.DMA((3, 7)),
        pltpu.SemaphoreType.DMA((3, 3, 6)),
        pltpu.SemaphoreType.DMA((3, 3, 6)),
    ]
    return shapes


def body(queries, cache_keys, cache_values, lengths, old_tiles, old_scales, slot_tiles):
    vmem = pl.BlockSpec(memory_space=pltpu.VMEM)
    return pl.pallas_call(
        kernel,
        out_shape=jax.ShapeDtypeStruct((8, 4096), jnp.bfloat16),
        in_specs=[
            vmem,
            pl.BlockSpec(memory_space=pltpu.SMEM),
            vmem,
            pl.BlockSpec(memory_space=pl.ANY),
            pl.BlockSpec(memory_space=pl.ANY),
            pl.BlockSpec(memory_space=pl.ANY),
            vmem,
        ],
        out_specs=vmem,
        scratch_shapes=scratch_shapes(),
        compiler_params=pltpu.CompilerParams(
            collective_id=0, has_side_effects=True, vmem_limit_bytes=58 * 2**20
        ),
    )(
        slot_tiles, lengths, queries[0], cache_keys[0], cache_values[0],
        old_tiles[0], old_scales[0],
    )


def solution(mesh):
    return jax.shard_map(
        body,
        mesh=mesh,
        in_specs=(
            P(("grp", "tp"), None, None),
            P(("grp", "tp"), None, None, None),
            P(("grp", "tp"), None, None, None),
            P(),
            P(("grp", "tp"), None, None, None),
            P(("grp", "tp"), None, None),
            P(),
        ),
        out_specs=P("tp", "grp"),
        check_vma=False,
    )
```
